256 devices in a mesh: elem: 64 (over y_lo, z, x), mode: 4 (over y_hi, core).
Axes of the slice: x: 4, y: 4 (y_hi: 2, y_lo: 2; y = y_hi * 2 + y_lo), z: 8, core: 2. Of those that a mesh axis runs over, the one named last changes fastest.
Arguments:
- velocity: float32 [3, 512, 65536], P(None, 'mode', 'elem'), may hold values from -6 to 6
- metric: float32 [4, 65536], P(None, 'elem'), may hold values from 0.5 to 2
- lift: float32 [1024, 32, 64], P('elem'), may hold values from -1.5 to 1.5
- blocks: float32 [1024, 32, 32], P('elem'), may hold values from -2.1 to 4, as said below
- conn: int32 [1024, 4], P('elem'), may hold values from 0 to 39, as said below
- send_list: int32 [64, 8], P('elem'), may hold values from 0 to 31, as said below
Outputs:
- velocity_new: float32 [3, 512, 65536], P(None, 'mode', 'elem')
- trace: float32 [2048, 8, 3, 512], P('elem', None, None, 'mode')
The draws below stay inside these ranges and needn't reach their ends.
Inputs may be any that keep to these rules, and one draw needn't show every extreme that they name: `blocks`: diagonal entries lie in 2 to 4, off-diagonal ones within -2.1 to 2.1. `conn`: rows d * 16 to (d + 1) * 16 - 1 belong to partition d. A slot below 32 is one of partition d's faces; slot 32 + k stands for face send_list[d - 1, k] of partition d - 1. Every slot of 32 to 39 is used by exactly one element of the partition, every face of the partition by one or two of its elements. `send_list`: row d holds 8 distinct faces of partition d, each used by exactly one of partition d's elements.
All inputs are finite; a program needn't handle non-finite values.
Results may differ from the reference program's by a relative error of at most 0.0001.
Values sent between devices are 32-bit elements; how exact they have to be, the bound alone decides.
No kernel may reach another device: no remote copies, remote signals or barrier semaphores. Data moves between devices by JAX's collectives and lax.ppermute only.
A program may use at most 64 MiB of HBM per device.

```python
import math
import jax
import jax.numpy as jnp
from jax import lax

PLANES = 512
NODES1 = 8
ROWS_E = 8
COLS_E = 2
SWEEPS = 8
NP = 64
E_DEV = 16
ELEMS = 1024
FACES = 2048
POINTS = 65536
N_ELEM = 64


def grid_tables(key):
    base = jax.random.fold_in(key, 7)
    partitions = ELEMS // E_DEV
    keys = jax.random.split(base, 3 * partitions)
    elem_total = COLS_E * ROWS_E
    face_total = 2 * elem_total
    perm_elem = jax.vmap(lambda one_key: jax.random.permutation(one_key, elem_total))(keys[0::3]).astype(jnp.int32)
    perm_face = jax.vmap(lambda one_key: jax.random.permutation(one_key, face_total))(keys[1::3]).astype(jnp.int32)
    perm_rows = jax.vmap(lambda one_key: jax.random.permutation(one_key, ROWS_E))(keys[2::3]).astype(jnp.int32)
    grid = jnp.arange(elem_total, dtype=jnp.int32)
    column = grid // ROWS_E
    row_of = grid % ROWS_E
    inverse_rows = jnp.argsort(perm_rows, axis=1, stable=True).astype(jnp.int32)
    prev_inverse = jnp.roll(inverse_rows, 1, axis=0)

    def one_partition(elem_perm, face_perm, prev_inv):
        right = face_perm[2 * grid]
        upper = face_perm[2 * grid + 1]
        left_inner = face_perm[jnp.maximum(2 * (grid - ROWS_E), 0)]
        left = jnp.where(column > 0, left_inner, face_total + prev_inv[row_of])
        below = face_perm[2 * (column * ROWS_E + (row_of - 1) % ROWS_E) + 1]
        rows_all = jnp.stack([right, upper, left, below], axis=1)
        return jnp.zeros((elem_total, 4), jnp.int32).at[elem_perm].set(rows_all)
    conn_all = jax.vmap(one_partition)(perm_elem, perm_face, prev_inverse)
    last_column = (COLS_E - 1) * ROWS_E
    sends = jax.vmap(lambda face_perm, row_perm: face_perm[2 * (last_column + row_perm)])(perm_face, perm_rows)
    return (conn_all.reshape(partitions * elem_total, 4).astype(jnp.int32), sends.astype(jnp.int32))


def draw_conn(key, part):
    return grid_tables(key)[0]


def draw_send_list(key, part):
    return grid_tables(key)[1]


def draw_blocks(key, part):
    block_width = 4 * NODES1
    first_key, second_key = jax.random.split(jax.random.fold_in(key, 11))
    offdiag = 0.35 * jnp.clip(jax.random.normal(first_key, (ELEMS, block_width, block_width), jnp.float32), -6.0, 6.0)
    diagonal = jax.random.uniform(second_key, (ELEMS, block_width), jnp.float32, 2.0, 4.0)
    eye_block = jnp.eye(block_width, dtype=jnp.float32)
    return offdiag * (1.0 - eye_block) + diagonal[:, :, None] * eye_block


def block_scale(rng, extent, cuts, least, largest):
    gain, own = 1.0, jax.random.fold_in(rng, 6)
    for axis_at, shards_of in cuts:
        draws = jnp.exp(jax.random.uniform(jax.random.fold_in(own, axis_at), (shards_of,), jnp.float32, least / len(cuts), largest / len(cuts)))
        gain = gain * jnp.repeat(draws, extent[axis_at] // shards_of).reshape([-1 if axis == axis_at else 1 for axis in range(len(extent))])
    return gain


def gaussian(stream_key, shape, deviation, reach, cuts=(), held_as=jnp.bfloat16):
    result = deviation * jax.random.normal(stream_key, shape, jnp.float32)
    if cuts:
        result = result * block_scale(stream_key, shape, cuts, -0.22, 0.18)
    return jnp.clip(result, -reach, reach).astype(held_as)


def setup_inputs(seed: int = 0) -> dict:
    key_list = jax.random.split(jax.random.key(seed), 7)
    velocity = gaussian(key_list[0], (3, PLANES, POINTS), 1.0, 6.0, ((1, 4), (2, 64)), jnp.float32)
    metric = jnp.clip(0.5 + 1.5 * jax.random.uniform(key_list[1], (4, POINTS), jnp.float32) ** block_scale(key_list[1], (4, POINTS), ((1, 64),), -0.2, 0.2), 0.5, 2.0)
    lift = gaussian(key_list[2], (ELEMS, 4 * NODES1, NP), 0.25, 1.5, ((0, 64),), jnp.float32)
    blocks = draw_blocks(jax.random.fold_in(key_list[6], 71), 0)
    conn = draw_conn(jax.random.fold_in(key_list[6], 71), 0)
    send_list = draw_send_list(jax.random.fold_in(key_list[6], 71), 0)
    return dict(velocity=velocity, metric=metric, lift=lift, blocks=blocks, conn=conn, send_list=send_list)


HIGHEST = lax.Precision.HIGHEST
TIME_STEP = 0.01
RELAXATION = 0.8
HELMHOLTZ_BASE = 0.5

def edge_derivative(length):
    index = jnp.arange(length, dtype=jnp.int32)
    points_at = jnp.cos(math.pi * index.astype(jnp.float32) / (length - 1))
    weights = jnp.where((index == 0) | (index == length - 1), 2.0, 1.0).astype(jnp.float32)
    parity = ((index[:, None] + index[None, :]) % 2).astype(jnp.float32)
    signs = 1.0 - 2.0 * parity
    diagonal_mask = index[:, None] == index[None, :]
    spacing = jnp.where(diagonal_mask, 1.0, points_at[:, None] - points_at[None, :])
    offdiag = jnp.where(diagonal_mask, 0.0, weights[:, None] / weights[None, :] * signs / spacing)
    return offdiag - jnp.diag(lax.optimization_barrier(jnp.sum(offdiag, axis=1)))

def node_tables(length):
    edge = edge_derivative(length)
    eye_edge = jnp.eye(length, dtype=jnp.float32)
    return (jnp.kron(eye_edge, edge), jnp.kron(edge, eye_edge))

def plane_tables(length):
    plane = jnp.arange(length, dtype=jnp.int32)[:, None]
    column = jnp.arange(length, dtype=jnp.int32)[None, :]
    wave = (column + 1) // 2
    phase = wave * plane % length
    angle = 2.0 * math.pi / length * phase.astype(jnp.float32)
    is_sine = (column % 2 == 0) & (column > 0)
    is_edge = (column == 0) | (column == length - 1)
    factor = jnp.where(is_edge, math.sqrt(1.0 / length), math.sqrt(2.0 / length)).astype(jnp.float32)
    rate = wave.astype(jnp.float32) * (8.0 / length)
    basis = factor * jnp.where(is_sine, jnp.sin(angle), jnp.cos(angle))
    slope = factor * rate * jnp.where(is_sine, jnp.cos(angle), -jnp.sin(angle))
    slope = jnp.where(column == length - 1, 0.0, slope)
    return (basis, slope, rate[0])

def reference(velocity, metric, lift, blocks, conn, send_list):
    planes = velocity.shape[1]
    share = E_DEV * NP
    face_nodes = NODES1
    basis, slope, rate = plane_tables(planes)
    along_r, along_s = node_tables(NODES1)
    kappa = HELMHOLTZ_BASE + rate * rate
    blocked_velocity = jnp.moveaxis(velocity.reshape(3, planes, N_ELEM, share), 2, 0)
    blocked_metric = jnp.moveaxis(metric.reshape(4, N_ELEM, share), 1, 0)

    def advect(inputs):
        coeffs, local_metric = inputs
        physical = jnp.einsum('pm,cmq->cpq', basis, coeffs, precision=HIGHEST)
        along_z = jnp.einsum('pm,cmq->cpq', slope, coeffs, precision=HIGHEST)
        grouped_nodes = physical.reshape(3, planes, share // NP, NP)
        by_r = jnp.einsum('kn,cpen->cpek', along_r, grouped_nodes, precision=HIGHEST).reshape(physical.shape)
        by_s = jnp.einsum('kn,cpen->cpek', along_s, grouped_nodes, precision=HIGHEST).reshape(physical.shape)
        grad_x = local_metric[0] * by_r + local_metric[1] * by_s
        grad_y = local_metric[2] * by_r + local_metric[3] * by_s
        nonlinear = physical[0] * grad_x + physical[1] * grad_y + physical[2] * along_z
        return jnp.einsum('pm,cpq->cmq', basis, nonlinear, precision=HIGHEST)
    advected = lax.map(advect, (blocked_velocity, blocked_metric))
    advected = jnp.moveaxis(advected, 0, 2).reshape(3, planes, POINTS)
    grouped = (velocity - TIME_STEP * advected).reshape(3, planes, ELEMS, NP)
    forcing_elem = jnp.einsum('ein,cmen->eicm', lift, grouped, precision=HIGHEST)
    owner = (jnp.arange(ELEMS, dtype=jnp.int32) // E_DEV)[:, None]
    before = jnp.maximum(owner - 1, 0)
    halo_index = jnp.clip(conn - 2 * E_DEV, 0, ROWS_E - 1)
    from_before = before * (2 * E_DEV) + send_list[before, halo_index]
    global_face = jnp.where(conn < 2 * E_DEV, owner * (2 * E_DEV) + conn, jnp.where(owner == 0, FACES, from_before)).astype(jnp.int32).reshape(-1)

    def assemble(per_elem):
        rows = per_elem.reshape((ELEMS * 4, face_nodes) + per_elem.shape[2:])
        return jax.ops.segment_sum(rows, global_face, num_segments=FACES + 1)[:FACES]

    def element_values(trace_now):
        padded = jnp.concatenate([trace_now, jnp.zeros((1,) + trace_now.shape[1:], jnp.float32)], axis=0)
        return padded[global_face].reshape(ELEMS, 4 * face_nodes, 3, planes)
    forcing = assemble(forcing_elem)
    diag_sum = assemble(jnp.diagonal(blocks, axis1=1, axis2=2))
    face_hits = jax.ops.segment_sum(jnp.ones((ELEMS * 4,), jnp.float32), global_face, num_segments=FACES + 1)[:FACES]
    diag_scale = diag_sum[:, :, None, None] + kappa * face_hits[:, None, None, None]
    trace = jnp.zeros((FACES, face_nodes, 3, planes), jnp.float32)
    for sweep_index in range(SWEEPS):
        values = element_values(trace)
        products = jnp.einsum('eij,ejcm->eicm', blocks, values, precision=HIGHEST) + kappa * values
        trace = trace + RELAXATION * (forcing - assemble(products)) / diag_scale
    values = element_values(trace)
    velocity_new = grouped + jnp.einsum('ein,eicm->cmen', lift, values, precision=HIGHEST)
    return (velocity_new.reshape(3, planes, POINTS), trace)
```

```python
import functools
import math

import jax
import jax.numpy as jnp
import ml_dtypes
import numpy as np
from jax import lax
from jax.experimental import pallas as pl
from jax.experimental.pallas import tpu as pltpu
from jax.sharding import PartitionSpec as P

NODES1 = 8
SWEEPS = 8
TIME_STEP = 0.01
RELAXATION = 0.8
HELMHOLTZ_BASE = 0.5
F32 = jnp.float32
BF16 = jnp.bfloat16
VMEM = pl.BlockSpec(memory_space=pltpu.VMEM)
SMEM = pl.BlockSpec(memory_space=pltpu.SMEM)


def split(x):
    high = x.astype(BF16)
    return high, (x - high.astype(F32)).astype(BF16)


def dot(a, b):
    return jnp.dot(a, b, preferred_element_type=F32)


def np_split(x):
    high = x.astype(np.float32).astype(ml_dtypes.bfloat16)
    low = (x - high.astype(np.float64)).astype(np.float32).astype(ml_dtypes.bfloat16)
    return high, low


def edge_derivative(length):
    index = np.arange(length)
    points_at = np.cos(math.pi * index / (length - 1))
    weights = np.where((index == 0) | (index == length - 1), 2.0, 1.0)
    signs = 1.0 - 2.0 * ((index[:, None] + index[None, :]) % 2)
    same = index[:, None] == index[None, :]
    spacing = np.where(same, 1.0, points_at[:, None] - points_at[None, :])
    offdiag = np.where(same, 0.0, weights[:, None] / weights[None, :] * signs / spacing)
    return offdiag - np.diag(offdiag.sum(axis=1))


def node_table(share):
    edge = edge_derivative(NODES1)
    eye = np.eye(NODES1)
    several = np.eye(share // (NODES1 * NODES1))
    along_r = np.kron(several, np.kron(eye, edge)).T
    along_s = np.kron(several, np.kron(edge, eye)).T
    high, low = np_split(np.concatenate([along_r, along_s], axis=1))
    return np.concatenate([high, high, low], axis=0)


def plane_tables(length):
    plane = np.arange(length)[:, None]
    column = np.arange(length)[None, :]
    wave = (column + 1) // 2
    angle = 2.0 * math.pi / length * (wave * plane % length)
    is_sine = (column % 2 == 0) & (column > 0)
    is_edge = (column == 0) | (column == length - 1)
    factor = np.where(is_edge, math.sqrt(1.0 / length), math.sqrt(2.0 / length))
    rate = wave * (8.0 / length)
    basis = factor * np.where(is_sine, np.sin(angle), np.cos(angle))
    slope = factor * rate * np.where(is_sine, np.cos(angle), -np.sin(angle))
    slope = np.where(column == length - 1, 0.0, slope)
    high, low = np_split(np.concatenate([basis, slope], axis=0))
    forward = np.concatenate([high, high, low], axis=1)
    high, low = np_split(basis.T)
    return forward, np.concatenate([high, high, low], axis=1)


def setup_kernel(info, conn, send, blocks, lift, abb, ai, abi, fh, fl, dgs, dgh, dgi, pos, a, f, dg):
    elem_count, width, node_count = lift.shape
    faces = 2 * elem_count
    halo = send.shape[0]
    edge = 2 * halo * NODES1
    total = a.shape[0]
    for face in range(faces):
        pos[face] = jnp.int32(-1)
    for k in range(halo):
        pos[send[k]] = jnp.int32(k)
    count = jnp.int32(2 * halo)
    for face in range(faces):
        now = pos[face]
        pos[face] = jnp.where(now < 0, count, now)
        count = count + jnp.where(now < 0, 1, 0)
    a[...] = jnp.zeros_like(a)
    f[...] = jnp.zeros_like(f)
    dg[...] = jnp.zeros_like(dg)
    lane = lax.broadcasted_iota(jnp.int32, (NODES1, total), 1)
    sub = lax.broadcasted_iota(jnp.int32, (NODES1, total), 0)
    eye = lax.broadcasted_iota(jnp.int32, (width, width), 0) == lax.broadcasted_iota(
        jnp.int32, (width, width), 1
    )
    first_half = lax.broadcasted_iota(jnp.int32, (width, 128), 1) < 64
    for e in range(elem_count):
        at, live = [], []
        for j in range(4):
            slot = conn[4 * e + j]
            own = slot < faces
            at.append(jnp.where(own, pos[jnp.minimum(slot, faces - 1)], slot - (faces - halo)))
            live.append(jnp.where(own | (info[0] > 0), 1.0, 0.0).astype(F32))
        place = jnp.concatenate(
            [jnp.where(lane == sub + NODES1 * at[j], live[j], 0.0) for j in range(4)], axis=0
        )
        block = blocks[e]
        rows = jnp.dot(block, place, precision=lax.Precision.HIGHEST, preferred_element_type=F32)
        diag = jnp.sum(jnp.where(eye, block, 0.0), axis=1, keepdims=True)
        diag = jnp.where(first_half, jnp.broadcast_to(diag, (width, 128)), 1.0)
        for j in range(4):
            here = pl.ds(pl.multiple_of(NODES1 * at[j], NODES1), NODES1)
            part = slice(NODES1 * j, NODES1 * (j + 1))
            nodes = slice(node_count * e, node_count * (e + 1))
            a[here, :] += live[j] * rows[part]
            dg[here, :] += live[j] * diag[part]
            f[here, nodes] += live[j] * lift[e, part, :]
    high, low = split(a[:edge, :edge])
    abb[...] = jnp.concatenate([high, high, low], axis=1)
    high, low = split(a[edge:, :])
    ai[...] = jnp.concatenate([high, high, low], axis=1)
    high, low = split(a[:edge, edge:])
    abi[...] = jnp.concatenate([high, high, low], axis=1)
    high, low = split(f[...])
    fh[...] = high
    fl[...] = low
    dgs[...] = dg[: edge // 2, :]
    dgh[...] = dg[edge // 2 : edge, :]
    dgi[...] = dg[edge:, :]


def weights_kernel(info, dgs, dgh, dgi, right, left, winv, keep):
    base = info[1] * 128
    wave = (lax.broadcasted_iota(jnp.int32, (1, 128), 1) + base + 1) // 2
    rate = wave.astype(F32) * info[2].astype(F32) ** -1 * 8.0
    kappa = HELMHOLTZ_BASE + rate * rate

    def put(rows, table):
        diag = jnp.broadcast_to(table[:, 0:1], table.shape)
        hits = kappa * jnp.broadcast_to(table[:, 64:65], table.shape)
        inverse = RELAXATION / (diag + hits)
        winv[rows, :] = inverse
        keep[rows, :] = 1.0 - inverse * hits

    half = dgs.shape[0]
    put(slice(0, half), dgs[...] + right[...])
    put(slice(half, 2 * half), dgh[...] + left[...])
    put(slice(2 * half, winv.shape[0]), dgi[...])


def advect_kernel(info, own, one, two, three, metric, forward, back, nodes, o0, o1, o2, o3, c3, n3):
    me = info[1]
    modes, share = own.shape[1], own.shape[2]
    planes = back.shape[0]
    for r, ref in enumerate((own, one, two, three)):
        row = pl.multiple_of((me ^ r) * modes, modes)
        for c in range(3):
            high, low = split(ref[c])
            lanes = slice(c * share, (c + 1) * share)
            c3[pl.ds(row, modes), lanes] = high
            c3[pl.ds(planes + row, modes), lanes] = low
            c3[pl.ds(2 * planes + row, modes), lanes] = high
    here = metric[:, pl.ds(pl.multiple_of(me * share, share), share)]
    rx, sx, ry, sy = (here[k : k + 1, :] for k in range(4))
    step = 128
    for start in range(0, planes, step):
        rows = slice(start, start + step)
        physical = dot(forward[rows, :], c3[...])
        along_z = dot(forward[planes + start : planes + start + step, :], c3[...])
        stacked = jnp.concatenate(
            [physical[:, c * share : (c + 1) * share] for c in range(3)], axis=0
        )
        high, low = split(stacked)
        slopes = dot(jnp.concatenate([high, low, high], axis=1), nodes[...])
        p0, p1, p2 = (physical[:, c * share : (c + 1) * share] for c in range(3))
        for c in range(3):
            lanes = slice(c * share, (c + 1) * share)
            by_r = slopes[c * step : (c + 1) * step, :share]
            by_s = slopes[c * step : (c + 1) * step, share:]
            term = p0 * (rx * by_r + sx * by_s) + p1 * (ry * by_r + sy * by_s)
            term = term + p2 * along_z[:, lanes]
            high, low = split(term)
            n3[start : start + step, lanes] = high
            n3[planes + start : planes + start + step, lanes] = low
            n3[2 * planes + start : 2 * planes + start + step, lanes] = high
    for r, ref in ((2, o2), (3, o3), (1, o1), (0, o0)):
        row = pl.multiple_of((me ^ r) * modes, modes)
        spectral = dot(back[pl.ds(row, modes), :], n3[...])
        for c in range(3):
            ref[c] = spectral[:, c * share : (c + 1) * share]


def triple(x):
    return jnp.concatenate([x, x, x], axis=1)


def stack(x):
    high, low = split(x)
    return jnp.concatenate([high, low, high], axis=0)


def forcing_kernel(info, velocity, own, one, two, three, fh, fl, winv, abi, rhs, fs, fi_w, fhalo, pib):
    me = info[1]
    share = own.shape[2]
    for r, ref in enumerate((own, one, two, three)):
        lanes = pl.ds(pl.multiple_of((me ^ r) * share, share), share)
        for c in range(3):
            rhs[c, :, lanes] = velocity[c, :, lanes] - TIME_STEP * ref[c]
    half = fs.shape[0]
    modes = rhs.shape[1]
    for c in range(3):
        high, low = split(rhs[c])
        nt = (((1,), (1,)), ((), ()))
        force = lax.dot_general(fh[...], high, nt, preferred_element_type=F32)
        force += lax.dot_general(fh[...], low, nt, preferred_element_type=F32)
        force += lax.dot_general(fl[...], high, nt, preferred_element_type=F32)
        lanes = slice(c * modes, (c + 1) * modes)
        fs[:, lanes] = force[:half]
        fhalo[:, lanes] = force[half : 2 * half]
        fi_w[:, lanes] = winv[2 * half :, :] * force[2 * half :]
    pib[...] = dot(abi[...], stack(fi_w[...]))


def first_kernel(fs, fhalo, right, left, winv, pib, abb, wfb, tb, ps, ph):
    half = fs.shape[0]
    force = jnp.concatenate([fs[...] + right[...], fhalo[...] + left[...]], axis=0)
    now = triple(winv[: 2 * half, :]) * force
    wfb[...] = now
    tb[...] = now
    out = dot(abb[...], stack(now)) + pib[...]
    ps[...] = out[:half]
    ph[...] = out[half:]


def edge_update(ps, ph, right, left, tb, winv, keep, wfb):
    half = ps.shape[0]
    product = jnp.concatenate([ps[...] + right[...], ph[...] + left[...]], axis=0)
    scale = triple(winv[: 2 * half, :])
    return triple(keep[: 2 * half, :]) * tb[...] + wfb[...] - scale * product


def edge_kernel(ps, ph, right, left, tb, winv, keep, wfb, pib, abb, tb_out, ps_out, ph_out):
    half = ps.shape[0]
    now = edge_update(ps, ph, right, left, tb, winv, keep, wfb)
    tb_out[...] = now
    out = dot(abb[...], stack(now)) + pib[...]
    ps_out[...] = out[:half]
    ph_out[...] = out[half:]


def inner_kernel(tb, ti, winv, keep, wfi, ai, abi, ti_out, pib_out):
    edge = tb.shape[0]
    product = dot(ai[...], stack(jnp.concatenate([tb[...], ti[...]], axis=0)))
    now = triple(keep[edge:, :]) * ti[...] + wfi[...] - triple(winv[edge:, :]) * product
    ti_out[...] = now
    pib_out[...] = dot(abi[...], stack(now))


def final_kernel(pos, ps, ph, right, left, tb, winv, keep, wfb, ti, rhs, fh, fl, out, trace, t):
    edge = tb.shape[0]
    modes = rhs.shape[1]
    t[:edge, :] = edge_update(ps, ph, right, left, tb, winv, keep, wfb)
    t[edge:, :] = ti[...]
    for face in range(trace.shape[0] // NODES1):
        row = pl.multiple_of(pos[face] * NODES1, NODES1)
        trace[face * NODES1 : (face + 1) * NODES1, :] = t[pl.ds(row, NODES1), :]
    for c in range(3):
        high, low = split(t[:, c * modes : (c + 1) * modes].T)
        add = dot(high, fh[...]) + dot(low, fh[...]) + dot(high, fl[...])
        out[c] = rhs[c] + add


def call(kernel, outs, *args, smem=(), smem_out=(), scratch=(), flops=0, limit=32):
    size = sum(x.size * x.dtype.itemsize for x in (*args, *outs))
    return pl.pallas_call(
        kernel,
        out_shape=tuple(outs),
        in_specs=[SMEM if k in smem else VMEM for k in range(len(args))],
        out_specs=tuple(SMEM if k in smem_out else VMEM for k in range(len(outs))),
        scratch_shapes=list(scratch),
        cost_estimate=pl.CostEstimate(flops=int(flops), bytes_accessed=int(size), transcendentals=0),
        compiler_params=pltpu.CompilerParams(vmem_limit_bytes=limit * 2**20),
    )(*args)


def arr(*shape, dtype=F32):
    return jax.ShapeDtypeStruct(shape, dtype)


def shards(velocity, metric, lift, blocks, conn, send_list):
    modes, points = velocity.shape[1:]
    ways = lax.axis_size("mode")
    planes = modes * ways
    share = points // ways
    elem_count = lift.shape[0]
    faces = 2 * elem_count
    halo = send_list.shape[1]
    half = halo * NODES1
    edge = 2 * half
    total = (faces + halo) * NODES1
    inner = total - edge
    cols = 3 * modes
    me = lax.axis_index("mode")
    part = lax.axis_index("elem")
    count = lax.axis_size("elem")
    ring = [(i, (i + 1) % count) for i in range(count)]
    back_ring = [(j, i) for i, j in ring]
    info = jnp.stack([part, me, jnp.int32(planes)]).astype(jnp.int32)

    def swap(x, r):
        return lax.ppermute(x, "mode", [(j, j ^ r) for j in range(ways)])

    def exchange(to_right, to_left):
        left = lax.ppermute(to_right, "elem", ring)
        right = lax.ppermute(to_left, "elem", back_ring)
        return right, left

    pieces = [lax.dynamic_slice_in_dim(velocity, (me ^ r) * share, share, 2) for r in range(ways)]
    got = {r: swap(pieces[r], r) for r in (2, 3, 1)}

    abb, ai, abi, fh, fl, dgs, dgh, dgi, pos = call(
        setup_kernel,
        [
            arr(edge, 3 * edge, dtype=BF16),
            arr(inner, 3 * total, dtype=BF16),
            arr(edge, 3 * inner, dtype=BF16),
            arr(total, points, dtype=BF16),
            arr(total, points, dtype=BF16),
            arr(half, 128),
            arr(half, 128),
            arr(inner, 128),
            arr(faces, dtype=jnp.int32),
        ],
        info,
        conn.reshape(-1),
        send_list.reshape(-1),
        blocks,
        lift,
        smem=(0, 1, 2),
        smem_out=(8,),
        scratch=[pltpu.VMEM((total, total), F32), pltpu.VMEM((total, points), F32), pltpu.VMEM((total, 128), F32)],
        flops=1e8,
    )
    right, left = exchange(dgs, dgh)
    winv, keep = call(
        weights_kernel, [arr(total, 128), arr(total, 128)], info, dgs, dgh, dgi, right, left, smem=(0,)
    )

    forward, back = plane_tables(planes)
    nodes = node_table(share)
    quarter = arr(3, modes, share)
    outs = call(
        advect_kernel,
        [quarter] * 4,
        info,
        pieces[0],
        got[1],
        got[2],
        got[3],
        metric,
        jnp.asarray(forward),
        jnp.asarray(back),
        jnp.asarray(nodes),
        smem=(0,),
        scratch=[pltpu.VMEM((3 * planes, 3 * share), BF16), pltpu.VMEM((3 * planes, 3 * share), BF16)],
        flops=5e9,
    )
    home = {r: swap(outs[r], r) for r in (2, 3, 1)}
    rhs, fs, wfi, fhalo, pib = call(
        forcing_kernel,
        [arr(3, modes, points), arr(half, cols), arr(inner, cols), arr(half, cols), arr(edge, cols)],
        info,
        velocity,
        outs[0],
        home[1],
        home[2],
        home[3],
        fh,
        fl,
        winv,
        abi,
        smem=(0,),
        flops=1e9,
    )
    right, left = exchange(fs, fhalo)
    edge_outs = [arr(edge, cols), arr(half, cols), arr(half, cols)]
    wfb, tb, ps, ph = call(
        first_kernel, [arr(edge, cols)] + edge_outs, fs, fhalo, right, left, winv, pib, abb, flops=1e8, limit=8
    )
    ti = wfi
    for sweep in range(2, SWEEPS + 1):
        right, left = exchange(ps, ph)
        ti, pib = call(
            inner_kernel,
            [arr(inner, cols), arr(edge, cols)],
            tb, ti, winv, keep, wfi, ai, abi,
            flops=3e8,
            limit=8,
        )
        if sweep < SWEEPS:
            tb, ps, ph = call(
                edge_kernel, edge_outs, ps, ph, right, left, tb, winv, keep, wfb, pib, abb, flops=1e8, limit=8
            )
    velocity_new, trace = call(
        final_kernel,
        [arr(3, modes, points), arr(faces * NODES1, cols)],
        pos, ps, ph, right, left, tb, winv, keep, wfb, ti, rhs, fh, fl,
        smem=(0,),
        scratch=[pltpu.VMEM((total, cols), F32)],
        flops=1e9,
    )
    return velocity_new, trace.reshape(faces, NODES1, 3, modes)


def solution(mesh):
    return jax.shard_map(
        shards,
        mesh=mesh,
        in_specs=(
            P(None, "mode", "elem"),
            P(None, "elem"),
            P("elem", None, None),
            P("elem", None, None),
            P("elem", None),
            P("elem", None),
        ),
        out_specs=(P(None, "mode", "elem"), P("elem", None, None, "mode")),
        check_vma=False,
    )
```

```python
import functools
import math

import jax
import jax.numpy as jnp
import ml_dtypes
import numpy as np
from jax import lax
from jax.experimental import pallas as pl
from jax.experimental.pallas import tpu as pltpu
from jax.sharding import PartitionSpec as P

NODES1 = 8
SWEEPS = 8
PLANES = 512
GROUP = 4
EDGE = 128
HALVES = 2
NODES = 384
TIME_STEP = 0.01
RELAXATION = 0.8
HELMHOLTZ_BASE = 0.5
F32 = jnp.float32
BF16 = jnp.bfloat16
VMEM = pl.BlockSpec(memory_space=pltpu.VMEM)
HBM = pl.BlockSpec(memory_space=pltpu.HBM)
SMEM = pl.BlockSpec(memory_space=pltpu.SMEM)


def split(x):
    high = x.astype(BF16)
    return high, (x - high.astype(F32)).astype(BF16)


def dot(a, b):
    return jnp.dot(a, b, preferred_element_type=F32)


def np_split(x):
    high = x.astype(np.float32).astype(ml_dtypes.bfloat16)
    low = (x - high.astype(np.float64)).astype(np.float32).astype(ml_dtypes.bfloat16)
    return high, low


def edge_derivative(length):
    index = np.arange(length)
    points_at = np.cos(math.pi * index / (length - 1))
    weights = np.where((index == 0) | (index == length - 1), 2.0, 1.0)
    signs = 1.0 - 2.0 * ((index[:, None] + index[None, :]) % 2)
    same = index[:, None] == index[None, :]
    spacing = np.where(same, 1.0, points_at[:, None] - points_at[None, :])
    offdiag = np.where(same, 0.0, weights[:, None] / weights[None, :] * signs / spacing)
    return offdiag - np.diag(offdiag.sum(axis=1))


def node_table(share):
    edge = edge_derivative(NODES1)
    eye = np.eye(NODES1)
    several = np.eye(share // (NODES1 * NODES1))
    along_r = np.kron(several, np.kron(eye, edge)).T
    along_s = np.kron(several, np.kron(edge, eye)).T
    high, low = np_split(np.concatenate([along_r, along_s], axis=1))
    return np.concatenate([high, high, low], axis=0)


def plane_tables(length):
    plane = np.arange(length)[:, None]
    column = np.arange(length)[None, :]
    wave = (column + 1) // 2
    angle = 2.0 * math.pi / length * (wave * plane % length)
    is_sine = (column % 2 == 0) & (column > 0)
    is_edge = (column == 0) | (column == length - 1)
    factor = np.where(is_edge, math.sqrt(1.0 / length), math.sqrt(2.0 / length))
    rate = wave * (8.0 / length)
    basis = factor * np.where(is_sine, np.sin(angle), np.cos(angle))
    slope = factor * rate * np.where(is_sine, np.cos(angle), -np.sin(angle))
    slope = np.where(column == length - 1, 0.0, slope)
    high, low = np_split(np.concatenate([basis, slope], axis=0))
    forward = np.concatenate([high, high, low], axis=1)
    high, low = np_split(basis.T)
    return forward, np.concatenate([high, high, low], axis=1)


def pack_kernel(conn, send, blocks, out):
    elem_count, width = blocks.shape[:2]
    for e in range(elem_count):
        parts = [blocks[e, NODES1 * j : NODES1 * (j + 1), :] for j in range(4)]
        out[NODES1 * e : NODES1 * (e + 1), :] = jnp.concatenate(parts, axis=1)
    lane = lax.broadcasted_iota(jnp.int32, (NODES1, 4 * width), 1)
    row = jnp.zeros_like(lane)
    numbers = [conn[e, j] for e in range(elem_count) for j in range(4)]
    numbers += [send[0, k] for k in range(send.shape[1])]
    for k, number in enumerate(numbers):
        row = jnp.where(lane == k, number, row)
    out[NODES1 * elem_count :, :] = row.astype(F32)


def setup_kernel(info, ints, packs, lift, ah, al, fh, fl, dgp, tie, pos, a, f, dg):
    elem_count, width, node_count = lift.shape
    faces = 2 * elem_count
    halo = faces // 4
    place = info[0] % GROUP
    lane = lax.broadcasted_iota(jnp.int32, (NODES1, NODES), 1)
    sub = lax.broadcasted_iota(jnp.int32, (NODES1, NODES), 0)
    diagonal = lax.broadcasted_iota(jnp.int32, (NODES1, width), 1)
    row_of = lax.broadcasted_iota(jnp.int32, (NODES1, width), 0)
    first_half = lax.broadcasted_iota(jnp.int32, (NODES1, 128), 1) < 64
    f[...] = jnp.zeros_like(f)

    def one(step, carry):
        r = GROUP - 1 - step
        p = (place + r) % GROUP
        whole = (info[0] - place + p) > 0
        base = r * 128
        for face in range(faces):
            pos[face] = jnp.int32(-1)
        for k in range(halo):
            pos[ints[base + 4 * elem_count + k]] = jnp.int32(k)
        count = jnp.int32(2 * halo)
        for face in range(faces):
            now = pos[face]
            pos[face] = jnp.where(now < 0, count, now)
            count = count + jnp.where(now < 0, 1, 0)
        a[...] = jnp.zeros_like(a)
        dg[...] = jnp.zeros_like(dg)
        for e in range(elem_count):
            at, live = [], []
            for j in range(4):
                slot = ints[base + 4 * e + j]
                own = slot < faces
                at.append(jnp.where(own, pos[jnp.minimum(slot, faces - 1)], slot - (faces - halo)))
                live.append(jnp.where(own | whole, 1.0, 0.0).astype(F32))
            spread = jnp.concatenate(
                [jnp.where(lane == sub + NODES1 * at[j], live[j], 0.0) for j in range(4)], axis=0
            )
            packed = packs[r, NODES1 * e : NODES1 * (e + 1), :]
            block = jnp.concatenate([packed[:, width * j : width * (j + 1)] for j in range(4)], axis=0)
            rows = jnp.dot(block, spread, precision=lax.Precision.HIGHEST, preferred_element_type=F32)
            for j in range(4):
                here = pl.ds(pl.multiple_of(NODES1 * at[j], NODES1), NODES1)
                part = slice(NODES1 * j, NODES1 * (j + 1))
                own_rows = block[part]
                diag = jnp.sum(
                    jnp.where(diagonal == row_of + NODES1 * j, own_rows, 0.0), axis=1, keepdims=True
                )
                diag = jnp.where(first_half, jnp.broadcast_to(diag, (NODES1, 128)), 1.0)
                a[here, :] += live[j] * rows[part]
                dg[here, :] += live[j] * diag

        high, low = split(a[...].T)
        ah[p] = high
        al[p] = low
        turned = dg[...].T
        dgp[p, 0:1, :] = turned[0:1]
        dgp[p, 1:2, :] = turned[64:65]
        return carry

    lax.fori_loop(0, GROUP, one, 0)
    quarter = elem_count // 4
    piece = quarter // HALVES
    for e in range(elem_count):
        q, rest = divmod(e, quarter)
        half, rest = divmod(rest, piece)
        column = ((half * 4 + q) * piece + rest) * node_count
        nodes = slice(column, column + node_count)
        for j in range(4):
            slot = ints[4 * e + j]
            own = slot < faces
            at = jnp.where(own, pos[jnp.minimum(slot, faces - 1)], slot - (faces - halo))
            live = jnp.where(own | (info[0] > 0), 1.0, 0.0).astype(F32)
            here = pl.ds(pl.multiple_of(NODES1 * at, NODES1), NODES1)
            part = slice(NODES1 * j, NODES1 * (j + 1))
            f[here, nodes] += live * lift[e, part, :]
    high, low = split(f[...])
    fh[...] = high
    fl[...] = low
    half = halo * NODES1
    last = ah[GROUP - 1, :half, :EDGE].astype(F32) + al[GROUP - 1, :half, :EDGE].astype(F32)
    first = ah[0, half:EDGE, :EDGE].astype(F32) + al[0, half:EDGE, :EDGE].astype(F32)
    tie[:half, :] = jnp.where(low_half(last), last, first)
    tie[half : half + NODES1, :] = jnp.where(
        low_half(dgp[0, :, :EDGE]), dgp[GROUP - 1, :, :EDGE], dgp[0, :, :EDGE]
    )


def low_half(x):
    return lax.broadcasted_iota(jnp.int32, x.shape, x.ndim - 1) < EDGE // 2


def meet(left, right):
    return pltpu.roll(jnp.where(low_half(left), left, right), EDGE // 2, 1)


def triple(x):
    return jnp.concatenate([x, x, x], axis=0)


def assemble(terms, before=None, after=None):
    zero = jnp.zeros_like(terms[0][:, :EDGE])
    sums = []
    for p, term in enumerate(terms):
        left = terms[p - 1][:, :EDGE] if p > 0 else (zero if before is None else before)
        right = terms[p + 1][:, :EDGE] if p < GROUP - 1 else (zero if after is None else after)
        sums.append(jnp.concatenate([term[:, :EDGE] + meet(left, right), term[:, EDGE:]], axis=1))
    return sums


def weights_kernel(info, dgp, tie_left, tie_right, winv, keep, bh, bl):
    half = EDGE // 2
    rows = winv.shape[1]
    base = info[1] * (rows * GROUP) + (info[0] % GROUP) * rows
    wave = (lax.broadcasted_iota(jnp.int32, (rows, 1), 0) + base + 1) // 2
    rate = wave.astype(F32) * (8.0 / PLANES)
    kappa = HELMHOLTZ_BASE + rate * rate
    sums = assemble([dgp[p] for p in range(GROUP)], tie_left[half:, :], tie_right[half:, :])
    for p in range(GROUP):
        diag = sums[p][0:1]
        hits = kappa * sums[p][1:2]
        diag = jnp.where(sums[p][1:2] > 0.0, diag, 1.0)
        inverse = RELAXATION / (diag + hits)
        winv[p] = inverse
        keep[p] = 1.0 - inverse * hits
    right = pltpu.roll(tie_right[:half, :], half, 1)
    left = pltpu.roll(tie_left[:half, :], half, 1)
    corner = jnp.concatenate(
        [jnp.where(low_half(right), right, 0.0), jnp.where(low_half(left), 0.0, left)], axis=0
    )
    high, low = split(corner)
    bh[...] = high
    bl[...] = low


def fetch_kernel(*refs):
    count = len(refs) // 2
    sems = refs[-1]
    copies = [pltpu.make_async_copy(refs[k], refs[count + k], sems.at[k]) for k in range(count)]
    for copy in copies:
        copy.start()
    for copy in copies:
        copy.wait()


def advect_kernel(half, info, own, one, two, three, metric, forward, back, nodes, o0, o1, o2, o3, c3, n3):
    me = info[1]
    modes, share = own.shape[1], own.shape[2]
    planes = back.shape[0]
    for r, ref in enumerate((own, one, two, three)):
        row = pl.multiple_of((me ^ r) * modes, modes)
        for c in range(3):
            high, low = split(ref[c])
            lanes = slice(c * share, (c + 1) * share)
            c3[pl.ds(row, modes), lanes] = high
            c3[pl.ds(planes + row, modes), lanes] = low
            c3[pl.ds(2 * planes + row, modes), lanes] = high
    here = metric[:, pl.ds(pl.multiple_of((me * HALVES + half) * share, share), share)]
    rx, sx, ry, sy = (here[k : k + 1, :] for k in range(4))
    step = 128
    for start in range(0, planes, step):
        rows = slice(start, start + step)
        physical = dot(forward[rows, :], c3[...])
        along_z = dot(forward[planes + start : planes + start + step, :], c3[...])
        stacked = jnp.concatenate(
            [physical[:, c * share : (c + 1) * share] for c in range(3)], axis=0
        )
        high, low = split(stacked)
        slopes = dot(jnp.concatenate([high, low, high], axis=1), nodes[...])
        p0, p1, p2 = (physical[:, c * share : (c + 1) * share] for c in range(3))
        for c in range(3):
            lanes = slice(c * share, (c + 1) * share)
            by_r = slopes[c * step : (c + 1) * step, :share]
            by_s = slopes[c * step : (c + 1) * step, share:]
            term = p0 * (rx * by_r + sx * by_s) + p1 * (ry * by_r + sy * by_s)
            term = term + p2 * along_z[:, lanes]
            high, low = split(term)
            n3[start : start + step, lanes] = high
            n3[planes + start : planes + start + step, lanes] = low
            n3[2 * planes + start : 2 * planes + start + step, lanes] = high
    for r, ref in ((2, o2), (3, o3), (1, o1), (0, o0)):
        row = pl.multiple_of((me ^ r) * modes, modes)
        spectral = dot(back[pl.ds(row, modes), :], n3[...])
        for c in range(3):
            ref[c] = spectral[:, c * share : (c + 1) * share]


def product(t, high_table, low_table):
    rows = t.shape[0]
    high, low = split(t)
    both = dot(jnp.concatenate([high, low], axis=0), high_table)
    return both[:rows] + both[rows:] + dot(high, low_table)


def lifted(half, info, velocity, pieces, fh, fl, rhs):
    share = pieces[0].shape[2]
    for r, ref in enumerate(pieces):
        at = info[1] ^ r
        there = pl.ds(pl.multiple_of((at * HALVES + half) * share, share), share)
        here = pl.ds(pl.multiple_of(at * share, share), share)
        for c in range(3):
            rhs[c, :, here] = velocity[c, :, there] - TIME_STEP * ref[c]
    nt = (((1,), (1,)), ((), ()))
    lanes = slice(half * rhs.shape[2], (half + 1) * rhs.shape[2])
    parts = []
    for c in range(3):
        high, low = split(rhs[c])
        total = lax.dot_general(high, fh[:, lanes], nt, preferred_element_type=F32)
        total += lax.dot_general(low, fh[:, lanes], nt, preferred_element_type=F32)
        total += lax.dot_general(high, fl[:, lanes], nt, preferred_element_type=F32)
        parts.append(total)
    return parts


def early_kernel(info, velocity, own, one, two, three, fh, fl, rhs, force):
    parts = lifted(0, info, velocity, (own, one, two, three), fh, fl, rhs)
    for c in range(3):
        force[c] = parts[c]


def forcing_kernel(info, velocity, own, one, two, three, fh, fl, before, rhs, f0, f1, f2, f3, force):
    place = info[0] % GROUP
    parts = lifted(1, info, velocity, (own, one, two, three), fh, fl, rhs)
    for c in range(3):
        force[c] = before[c] + parts[c]
    rows = f0.shape[0] // 3
    for r, ref in enumerate((f0, f1, f2, f3)):
        at = pl.ds(pl.multiple_of(((place + r) % GROUP) * rows, rows), rows)
        for c in range(3):
            ref[c * rows : (c + 1) * rows, :] = force[c, at, :]


def ends(first, last):
    return jnp.where(low_half(last), last, first)


def ahead(t, ah, al):
    first = product(t[0], ah[0, :, :EDGE], al[0, :, :EDGE])
    last = product(t[GROUP - 1], ah[GROUP - 1, :, :EDGE], al[GROUP - 1, :, :EDGE])
    return ends(first, last)


def advance(t, winv, keep, wf, ah, al, t_out):
    terms = [product(t[p], ah[p], al[p]) for p in range(GROUP)]
    for p, total in enumerate(assemble(terms)):
        t_out[p] = triple(keep[p]) * t[p] + wf[p] - triple(winv[p]) * total
    return terms


def start_kernel(info, f0, f1, f2, f3, winv, ah, al, wf, t_out, message, gather):
    place = info[0] % GROUP
    for r, ref in enumerate((f0, f1, f2, f3)):
        gather[(place + GROUP - r) % GROUP] = ref[...]
    terms = [gather[p] for p in range(GROUP)]
    message[:, :EDGE] = ends(terms[0][:, :EDGE], terms[GROUP - 1][:, :EDGE])
    for p, total in enumerate(assemble(terms)):
        now = triple(winv[p]) * total
        wf[p] = now
        t_out[p] = now
    message[:, EDGE:] = ahead(t_out, ah, al)


def inner_kernel(t, winv, keep, wf, ah, al, t_out):
    advance(t, winv, keep, wf, ah, al, t_out)


def correct(sign, t, message, left, right, winv, keep, ah, al, bh, bl):
    scale = sign * triple(ends(winv[0, :, :EDGE], winv[GROUP - 1, :, :EDGE]))
    hold = triple(ends(keep[0, :, :EDGE], keep[GROUP - 1, :, :EDGE]))
    share = scale * meet(left[:, :EDGE], right[:, :EDGE])
    theirs = scale * message[:, :EDGE]
    late = meet(left[:, EDGE:], right[:, EDGE:]) + product(theirs, bh[...], bl[...])
    low = low_half(share)
    share_last = jnp.where(low, share, 0.0)
    share_first = jnp.where(low, 0.0, share)
    none = jnp.zeros((share.shape[0], NODES), F32)
    terms = [none] * GROUP
    terms[0] = product(share_first, ah[0, :EDGE, :], al[0, :EDGE, :])
    terms[GROUP - 1] = product(share_last, ah[GROUP - 1, :EDGE, :], al[GROUP - 1, :EDGE, :])
    sums = assemble(terms)
    add = hold * share - sign * scale * late
    if sign > 0:
        add = add + share
    parts = [jnp.where(low, 0.0, add)] + [None] * (GROUP - 2) + [jnp.where(low, add, 0.0)]
    result = []
    for p in range(GROUP):
        now = t[p] - triple(winv[p]) * sums[p]
        if parts[p] is not None:
            now = jnp.concatenate([now[:, :EDGE] + parts[p], now[:, EDGE:]], axis=1)
        result.append(now)
    return result, share


def sweep_kernel(t, message, left, right, winv, keep, wf, ah, al, bh, bl, t_out, out_message, now):
    result, _ = correct(-1.0, t, message, left, right, winv, keep, ah, al, bh, bl)
    send_on(result, winv, keep, wf, ah, al, t_out, out_message, now)


def send_on(result, winv, keep, wf, ah, al, t_out, out_message, now):
    for p in range(GROUP):
        now[p] = result[p]
    terms = advance(now, winv, keep, wf, ah, al, t_out)
    out_message[:, :EDGE] = ends(terms[0][:, :EDGE], terms[GROUP - 1][:, :EDGE])
    out_message[:, EDGE:] = ahead(t_out, ah, al)


def second_kernel(t, message, left, right, winv, keep, wf, ah, al, bh, bl, t_out, out_message, wf_out, now):
    result, share = correct(1.0, t, message, left, right, winv, keep, ah, al, bh, bl)
    low = low_half(share)
    for p in range(GROUP):
        wf_out[p] = wf[p]
    wf_out[0, :, :EDGE] += jnp.where(low, 0.0, share)
    wf_out[GROUP - 1, :, :EDGE] += jnp.where(low, share, 0.0)
    send_on(result, winv, keep, wf_out, ah, al, t_out, out_message, now)


def last_kernel(info, t, message, left, right, winv, keep, ah, al, bh, bl, o0, o1, o2, o3, now):
    result, _ = correct(-1.0, t, message, left, right, winv, keep, ah, al, bh, bl)
    for p in range(GROUP):
        now[p] = result[p]
    place = info[0] % GROUP
    for r, ref in enumerate((o0, o1, o2, o3)):
        ref[...] = now[(place + r) % GROUP]


def final_kernel(info, pos, t0, t1, t2, t3, rhs0, rhs1, fh, fl, out, trace, t, turned):
    place = info[0] % GROUP
    modes, width = rhs0.shape[1:]
    rows = t0.shape[0] // 3
    share = width // 4
    for r, ref in enumerate((t0, t1, t2, t3)):
        at = pl.ds(pl.multiple_of(((place + GROUP - r) % GROUP) * rows, rows), rows)
        for c in range(3):
            t[c, at, :] = ref[c * rows : (c + 1) * rows, :]
    for c in range(3):
        high, low = split(t[c])
        both = dot(jnp.concatenate([high, low], axis=0), fh[...])
        both = both[:modes] + both[modes:] + dot(high, fl[...])
        for half, rhs in enumerate((rhs0, rhs1)):
            for q in range(4):
                lanes = slice((q * HALVES + half) * share, (q * HALVES + half + 1) * share)
                here = slice(q * share, (q + 1) * share)
                from_t = both[:, half * width + q * share : half * width + (q + 1) * share]
                out[c, :, lanes] = rhs[c, :, here] + from_t
        turned[:, c * modes : (c + 1) * modes] = t[c].T
    for face in range(trace.shape[0] // NODES1):
        row = pl.multiple_of(pos[face] * NODES1, NODES1)
        trace[face * NODES1 : (face + 1) * NODES1, :] = turned[pl.ds(row, NODES1), :]


def call(kernel, outs, *args, smem=(), smem_out=(), hbm=(), scratch=(), flops=0, limit=32):
    size = sum(x.size * x.dtype.itemsize for x in (*args, *outs))
    return pl.pallas_call(
        kernel,
        out_shape=tuple(outs),
        in_specs=[SMEM if k in smem else HBM if k in hbm else VMEM for k in range(len(args))],
        out_specs=tuple(SMEM if k in smem_out else VMEM for k in range(len(outs))),
        scratch_shapes=list(scratch),
        cost_estimate=pl.CostEstimate(flops=int(flops), bytes_accessed=int(size), transcendentals=0),
        compiler_params=pltpu.CompilerParams(vmem_limit_bytes=limit * 2**20),
    )(*args)


def arr(*shape, dtype=F32):
    return jax.ShapeDtypeStruct(shape, dtype)


def shards(velocity, metric, lift, blocks, conn, send_list):
    modes, points = velocity.shape[1:]
    ways = lax.axis_size("mode")
    planes = modes * ways
    share = points // ways
    elem_count, width = lift.shape[:2]
    faces = 2 * elem_count
    half = EDGE // 2
    rows = 3 * modes // GROUP
    me = lax.axis_index("mode")
    part = lax.axis_index("elem")
    count = lax.axis_size("elem")
    info = jnp.stack([part, me]).astype(jnp.int32)

    def swap(x, r):
        return lax.ppermute(x, "mode", [(j, j ^ r) for j in range(ways)])

    def turn(x, r):
        pairs = [(i, i - i % GROUP + (i + r) % GROUP) for i in range(count)]
        return lax.ppermute(x, "elem", pairs)

    def exchange(x):
        left = lax.ppermute(x, "elem", [(i, (i + GROUP) % count) for i in range(count)])
        right = lax.ppermute(x, "elem", [((i + GROUP) % count, i) for i in range(count)])
        return left, right

    size = share // HALVES
    chunk = arr(3, modes, size)

    def cut(r, h):
        return lax.dynamic_slice_in_dim(velocity, ((me ^ r) * HALVES + h) * size, size, 2)

    got = [{r: cut(r, h) for r in range(ways)} for h in range(HALVES)]
    for h in range(HALVES):
        for r in (2, 3):
            got[h][r] = swap(got[h][r], r)
    got[0][1] = swap(got[0][1], 1)

    (packed,) = call(
        pack_kernel,
        [arr(elem_count * NODES1 + NODES1, 4 * width)],
        conn, send_list, blocks,
        smem=(0, 1),
        limit=4,
    )
    packed, got[0][1] = lax.optimization_barrier((packed, got[0][1]))
    packs = jnp.stack([packed, turn(packed, GROUP - 1)])
    packs = jnp.concatenate([packs, turn(packs, 2)])
    packs, theirs = lax.optimization_barrier((packs, got[1][1]))
    got[1][1] = swap(theirs, 1)
    ints = packs[:, -NODES1, :].astype(jnp.int32).reshape(-1)
    tables = [jnp.asarray(x) for x in (*plane_tables(planes), node_table(share // HALVES))]
    tables = call(
        fetch_kernel,
        [arr(*x.shape, dtype=BF16) for x in tables],
        *tables,
        hbm=(0, 1, 2),
        scratch=[pltpu.SemaphoreType.DMA((3,))],
        limit=4,
    )
    home = []
    for h in range(HALVES):
        outs = call(
            functools.partial(advect_kernel, h),
            [chunk] * 4,
            info,
            *(got[h][r] for r in range(4)),
            metric,
            *tables,
            smem=(0,),
            scratch=[pltpu.VMEM((3 * planes, 3 * share // HALVES), BF16)] * 2,
            flops=4e9,
            limit=12,
        )
        home.append({0: outs[0]})
        for r in (2, 3, 1):
            home[h][r] = swap(outs[r], r)
        if h == 0:
            continue
        packs, home[h][0] = lax.optimization_barrier((packs, home[h][0]))
        ah, al, fh, fl, dgp, tie, pos = call(
            setup_kernel,
            [
                arr(GROUP, NODES, NODES, dtype=BF16),
                arr(GROUP, NODES, NODES, dtype=BF16),
                arr(NODES, points, dtype=BF16),
                arr(NODES, points, dtype=BF16),
                arr(GROUP, NODES1, NODES),
                arr(half + NODES1, EDGE),
                arr(faces, dtype=jnp.int32),
            ],
            info,
            ints,
            packs,
            lift,
            smem=(0, 1),
            smem_out=(6,),
            scratch=[pltpu.VMEM((NODES, NODES), F32), pltpu.VMEM((NODES, points), F32), pltpu.VMEM((NODES, 128), F32)],
            flops=8e9,
            limit=10,
        )
    piece = arr(rows, NODES)
    rhs_part = arr(3, modes, points // HALVES)
    rhs0, early = call(
        early_kernel,
        [rhs_part, arr(3, modes, NODES)],
        info, velocity, *(home[0][r] for r in range(4)), fh, fl,
        smem=(0,),
        flops=1.7e9,
        limit=10,
    )
    rhs1, *force = call(
        forcing_kernel,
        [rhs_part] + [piece] * GROUP,
        info, velocity, *(home[1][r] for r in range(4)), fh, fl, early,
        smem=(0,),
        scratch=[pltpu.VMEM((3, modes, NODES), F32)],
        flops=1.7e9,
        limit=10,
    )
    moved = {r: turn(force[r], r) for r in (2, 1, 3)}
    tie, force[0] = lax.optimization_barrier((tie, force[0]))
    tie_left, tie_right = exchange(tie)
    winv, keep, bh, bl = call(
        weights_kernel,
        [arr(GROUP, rows // 3, NODES)] * 2 + [arr(EDGE, EDGE, dtype=BF16)] * 2,
        info, dgp, tie_left, tie_right,
        smem=(0,),
        limit=8,
    )

    state = arr(GROUP, rows, NODES)
    note = arr(rows, 2 * EDGE)
    scratch = [pltpu.VMEM((GROUP, rows, NODES), F32)]
    wf, t, message = call(
        start_kernel,
        [state, state, note],
        info, force[0], moved[1], moved[2], moved[3], winv, ah, al,
        smem=(0,),
        scratch=scratch,
        flops=1e8,
        limit=8,
    )
    for pair in range(SWEEPS // 2):
        left, right = exchange(message)
        (t,) = call(inner_kernel, [state], t, winv, keep, wf, ah, al, flops=3e8, limit=8)
        if pair == SWEEPS // 2 - 1:
            break
        args = (t, message, left, right, winv, keep, wf, ah, al, bh, bl)
        if pair == 0:
            t, message, wf = call(
                second_kernel, [state, note, state], *args, scratch=scratch, flops=4e8, limit=8
            )
        else:
            t, message = call(sweep_kernel, [state, note], *args, scratch=scratch, flops=4e8, limit=8)
    ends_out = call(
        last_kernel,
        [piece] * GROUP,
        info, t, message, left, right, winv, keep, ah, al, bh, bl,
        smem=(0,),
        scratch=scratch,
        flops=1e8,
        limit=8,
    )
    there = {r: turn(ends_out[r], r) for r in (2, 1, 3)}
    velocity_new, trace = call(
        final_kernel,
        [arr(3, modes, points), arr(faces * NODES1, 3 * modes)],
        info, pos, ends_out[0], there[1], there[2], there[3], rhs0, rhs1, fh, fl,
        smem=(0, 1),
        scratch=[pltpu.VMEM((3, modes, NODES), F32), pltpu.VMEM((NODES, 3 * modes), F32)],
        flops=1e9,
        limit=10,
    )
    return velocity_new, trace.reshape(faces, NODES1, 3, modes)


def solution(mesh):
    return jax.shard_map(
        shards,
        mesh=mesh,
        in_specs=(
            P(None, "mode", "elem"),
            P(None, "elem"),
            P("elem", None, None),
            P("elem", None, None),
            P("elem", None),
            P("elem", None),
        ),
        out_specs=(P(None, "mode", "elem"), P("elem", None, None, "mode")),
        check_vma=False,
    )
```

```python
import functools
import math

import jax
import jax.numpy as jnp
import ml_dtypes
import numpy as np
from jax import lax
from jax.experimental import pallas as pl
from jax.experimental.pallas import tpu as pltpu
from jax.sharding import PartitionSpec as P

NODES1 = 8
SWEEPS = 8
PLANES = 512
GROUP = 4
EDGE = 128
HALVES = 2
NODES = 384
TIME_STEP = 0.01
RELAXATION = 0.8
HELMHOLTZ_BASE = 0.5
F32 = jnp.float32
BF16 = jnp.bfloat16
VMEM = pl.BlockSpec(memory_space=pltpu.VMEM)
HBM = pl.BlockSpec(memory_space=pltpu.HBM)
SMEM = pl.BlockSpec(memory_space=pltpu.SMEM)


def split(x):
    high = x.astype(BF16)
    return high, (x - high.astype(F32)).astype(BF16)


def dot(a, b):
    return jnp.dot(a, b, preferred_element_type=F32)


def np_split(x):
    high = x.astype(np.float32).astype(ml_dtypes.bfloat16)
    low = (x - high.astype(np.float64)).astype(np.float32).astype(ml_dtypes.bfloat16)
    return high, low


def edge_derivative(length):
    index = np.arange(length)
    points_at = np.cos(math.pi * index / (length - 1))
    weights = np.where((index == 0) | (index == length - 1), 2.0, 1.0)
    signs = 1.0 - 2.0 * ((index[:, None] + index[None, :]) % 2)
    same = index[:, None] == index[None, :]
    spacing = np.where(same, 1.0, points_at[:, None] - points_at[None, :])
    offdiag = np.where(same, 0.0, weights[:, None] / weights[None, :] * signs / spacing)
    return offdiag - np.diag(offdiag.sum(axis=1))


def node_table(share):
    edge = edge_derivative(NODES1)
    eye = np.eye(NODES1)
    several = np.eye(share // (NODES1 * NODES1))
    along_r = np.kron(several, np.kron(eye, edge)).T
    along_s = np.kron(several, np.kron(edge, eye)).T
    return np_split(np.concatenate([along_r, along_s], axis=1))


def plane_tables(length):
    plane = np.arange(length)[:, None]
    column = np.arange(length)[None, :]
    wave = (column + 1) // 2
    angle = 2.0 * math.pi / length * (wave * plane % length)
    is_sine = (column % 2 == 0) & (column > 0)
    is_edge = (column == 0) | (column == length - 1)
    factor = np.where(is_edge, math.sqrt(1.0 / length), math.sqrt(2.0 / length))
    rate = wave * (8.0 / length)
    basis = factor * np.where(is_sine, np.sin(angle), np.cos(angle))
    slope = factor * rate * np.where(is_sine, np.cos(angle), -np.sin(angle))
    slope = np.where(column == length - 1, 0.0, slope)
    return (*np_split(np.concatenate([basis, slope], axis=0)), *np_split(basis.T))


def pack_kernel(conn, send, blocks, out):
    elem_count, width = blocks.shape[:2]
    for e in range(elem_count):
        parts = [blocks[e, NODES1 * j : NODES1 * (j + 1), :] for j in range(4)]
        out[NODES1 * e : NODES1 * (e + 1), :] = jnp.concatenate(parts, axis=1)
    lane = lax.broadcasted_iota(jnp.int32, (NODES1, 4 * width), 1)
    row = jnp.zeros_like(lane)
    numbers = [conn[e, j] for e in range(elem_count) for j in range(4)]
    numbers += [send[0, k] for k in range(send.shape[1])]
    for k, number in enumerate(numbers):
        row = jnp.where(lane == k, number, row)
    out[NODES1 * elem_count :, :] = row.astype(F32)


def lift_kernel(info, conn, send, lift, fh, fl, pos, f):
    elem_count, _, node_count = lift.shape
    faces = 2 * elem_count
    halo = send.shape[1]
    for face in range(faces):
        pos[face] = jnp.int32(-1)
    for k in range(halo):
        pos[send[0, k]] = jnp.int32(k)
    count = jnp.int32(2 * halo)
    for face in range(faces):
        now = pos[face]
        pos[face] = jnp.where(now < 0, count, now)
        count = count + jnp.where(now < 0, 1, 0)
    f[...] = jnp.zeros_like(f)
    quarter = elem_count // 4
    piece = quarter // HALVES
    for e in range(elem_count):
        q, rest = divmod(e, quarter)
        half, rest = divmod(rest, piece)
        column = ((half * 4 + q) * piece + rest) * node_count
        nodes = slice(column, column + node_count)
        for j in range(4):
            slot = conn[e, j]
            own = slot < faces
            at = jnp.where(own, pos[jnp.minimum(slot, faces - 1)], slot - (faces - halo))
            live = jnp.where(own | (info[0] > 0), 1.0, 0.0).astype(F32)
            here = pl.ds(pl.multiple_of(NODES1 * at, NODES1), NODES1)
            part = slice(NODES1 * j, NODES1 * (j + 1))
            f[here, nodes] += live * lift[e, part, :]
    high, low = split(f[...])
    fh[...] = high
    fl[...] = low


def setup_kernel(info, ints, packs, ah, al, dgp, tie, pos, a, dg):
    width = packs.shape[2] // 4
    elem_count = packs.shape[1] // NODES1 - 1
    faces = 2 * elem_count
    halo = faces // 4
    place = info[0] % GROUP
    lane = lax.broadcasted_iota(jnp.int32, (NODES1, NODES), 1)
    sub = lax.broadcasted_iota(jnp.int32, (NODES1, NODES), 0)
    diagonal = lax.broadcasted_iota(jnp.int32, (NODES1, width), 1)
    row_of = lax.broadcasted_iota(jnp.int32, (NODES1, width), 0)
    first_half = lax.broadcasted_iota(jnp.int32, (NODES1, 128), 1) < 64

    def one(step, carry):
        r = GROUP - 1 - step
        p = (place + r) % GROUP
        whole = (info[0] - place + p) > 0
        base = r * 128
        for face in range(faces):
            pos[face] = jnp.int32(-1)
        for k in range(halo):
            pos[ints[base + 4 * elem_count + k]] = jnp.int32(k)
        count = jnp.int32(2 * halo)
        for face in range(faces):
            now = pos[face]
            pos[face] = jnp.where(now < 0, count, now)
            count = count + jnp.where(now < 0, 1, 0)
        a[...] = jnp.zeros_like(a)
        dg[...] = jnp.zeros_like(dg)
        for e in range(elem_count):
            at, live = [], []
            for j in range(4):
                slot = ints[base + 4 * e + j]
                own = slot < faces
                at.append(jnp.where(own, pos[jnp.minimum(slot, faces - 1)], slot - (faces - halo)))
                live.append(jnp.where(own | whole, 1.0, 0.0).astype(F32))
            spread = jnp.concatenate(
                [jnp.where(lane == sub + NODES1 * at[j], live[j], 0.0) for j in range(4)], axis=0
            )
            packed = packs[r, NODES1 * e : NODES1 * (e + 1), :]
            block = jnp.concatenate([packed[:, width * j : width * (j + 1)] for j in range(4)], axis=0)
            rows = jnp.dot(block, spread, precision=lax.Precision.HIGHEST, preferred_element_type=F32)
            for j in range(4):
                here = pl.ds(pl.multiple_of(NODES1 * at[j], NODES1), NODES1)
                part = slice(NODES1 * j, NODES1 * (j + 1))
                own_rows = block[part]
                diag = jnp.sum(
                    jnp.where(diagonal == row_of + NODES1 * j, own_rows, 0.0), axis=1, keepdims=True
                )
                diag = jnp.where(first_half, jnp.broadcast_to(diag, (NODES1, 128)), 1.0)
                a[here, :] += live[j] * rows[part]
                dg[here, :] += live[j] * diag

        high, low = split(a[...].T)
        ah[p] = high
        al[p] = low
        turned = dg[...].T
        dgp[p, 0:1, :] = turned[0:1]
        dgp[p, 1:2, :] = turned[64:65]
        return carry

    lax.fori_loop(0, GROUP, one, 0)
    half = halo * NODES1
    last = ah[GROUP - 1, :half, :EDGE].astype(F32) + al[GROUP - 1, :half, :EDGE].astype(F32)
    first = ah[0, half:EDGE, :EDGE].astype(F32) + al[0, half:EDGE, :EDGE].astype(F32)
    tie[:half, :] = jnp.where(low_half(last), last, first)
    tie[half : half + NODES1, :] = jnp.where(
        low_half(dgp[0, :, :EDGE]), dgp[GROUP - 1, :, :EDGE], dgp[0, :, :EDGE]
    )


def low_half(x):
    return lax.broadcasted_iota(jnp.int32, x.shape, x.ndim - 1) < EDGE // 2


def meet(left, right):
    return pltpu.roll(jnp.where(low_half(left), left, right), EDGE // 2, 1)


def triple(x):
    return jnp.concatenate([x, x, x], axis=0)


def assemble(terms, before=None, after=None):
    zero = jnp.zeros_like(terms[0][:, :EDGE])
    sums = []
    for p, term in enumerate(terms):
        left = terms[p - 1][:, :EDGE] if p > 0 else (zero if before is None else before)
        right = terms[p + 1][:, :EDGE] if p < GROUP - 1 else (zero if after is None else after)
        sums.append(jnp.concatenate([term[:, :EDGE] + meet(left, right), term[:, EDGE:]], axis=1))
    return sums


def weights_kernel(info, dgp, tie_left, tie_right, winv, keep, bh, bl):
    half = EDGE // 2
    rows = winv.shape[1]
    base = info[1] * (rows * GROUP) + (info[0] % GROUP) * rows
    wave = (lax.broadcasted_iota(jnp.int32, (rows, 1), 0) + base + 1) // 2
    rate = wave.astype(F32) * (8.0 / PLANES)
    kappa = HELMHOLTZ_BASE + rate * rate
    sums = assemble([dgp[p] for p in range(GROUP)], tie_left[half:, :], tie_right[half:, :])
    for p in range(GROUP):
        diag = sums[p][0:1]
        hits = kappa * sums[p][1:2]
        diag = jnp.where(sums[p][1:2] > 0.0, diag, 1.0)
        inverse = RELAXATION / (diag + hits)
        winv[p] = inverse
        keep[p] = 1.0 - inverse * hits
    right = pltpu.roll(tie_right[:half, :], half, 1)
    left = pltpu.roll(tie_left[:half, :], half, 1)
    corner = jnp.concatenate(
        [jnp.where(low_half(right), right, 0.0), jnp.where(low_half(left), 0.0, left)], axis=0
    )
    high, low = split(corner)
    bh[...] = high
    bl[...] = low


def fetch_kernel(forward_high, forward_low, back_high, back_low, high, low, forward, back, nodes, sems):
    copies = []
    for first, second, out in ((forward_high, forward_low, forward), (back_high, back_low, back)):
        size = first.shape[1]
        for k, table in enumerate((first, first, second)):
            there = out.at[:, k * size : (k + 1) * size]
            copies.append(pltpu.make_async_copy(table, there, sems.at[len(copies)]))
    size = high.shape[0]
    for k, table in enumerate((high, high, low)):
        there = nodes.at[k * size : (k + 1) * size, :]
        copies.append(pltpu.make_async_copy(table, there, sems.at[len(copies)]))
    for copy in copies:
        copy.start()
    for copy in copies:
        copy.wait()


def advect_kernel(half, info, own, one, two, three, metric, forward, back, nodes, o0, o1, o2, o3, c3, n3):
    me = info[1]
    modes, share = own.shape[1], own.shape[2]
    planes = back.shape[0]
    for r, ref in enumerate((own, one, two, three)):
        row = pl.multiple_of((me ^ r) * modes, modes)
        for c in range(3):
            high, low = split(ref[c])
            lanes = slice(c * share, (c + 1) * share)
            c3[pl.ds(row, modes), lanes] = high
            c3[pl.ds(planes + row, modes), lanes] = low
            c3[pl.ds(2 * planes + row, modes), lanes] = high
    here = metric[:, pl.ds(pl.multiple_of((me * HALVES + half) * share, share), share)]
    rx, sx, ry, sy = (here[k : k + 1, :] for k in range(4))
    step = 128
    for start in range(0, planes, step):
        rows = slice(start, start + step)
        physical = dot(forward[rows, :], c3[...])
        along_z = dot(forward[planes + start : planes + start + step, :], c3[...])
        stacked = jnp.concatenate(
            [physical[:, c * share : (c + 1) * share] for c in range(3)], axis=0
        )
        high, low = split(stacked)
        slopes = dot(jnp.concatenate([high, low, high], axis=1), nodes[...])
        p0, p1, p2 = (physical[:, c * share : (c + 1) * share] for c in range(3))
        for c in range(3):
            lanes = slice(c * share, (c + 1) * share)
            by_r = slopes[c * step : (c + 1) * step, :share]
            by_s = slopes[c * step : (c + 1) * step, share:]
            term = p0 * (rx * by_r + sx * by_s) + p1 * (ry * by_r + sy * by_s)
            term = term + p2 * along_z[:, lanes]
            high, low = split(term)
            n3[start : start + step, lanes] = high
            n3[planes + start : planes + start + step, lanes] = low
            n3[2 * planes + start : 2 * planes + start + step, lanes] = high
    for r, ref in ((2, o2), (3, o3), (1, o1), (0, o0)):
        row = pl.multiple_of((me ^ r) * modes, modes)
        spectral = dot(back[pl.ds(row, modes), :], n3[...])
        for c in range(3):
            ref[c] = spectral[:, c * share : (c + 1) * share]


def product(t, high_table, low_table):
    rows = t.shape[0]
    high, low = split(t)
    both = dot(jnp.concatenate([high, low], axis=0), high_table)
    return both[:rows] + both[rows:] + dot(high, low_table)


def lifted(half, info, velocity, pieces, fh, fl, rhs):
    share = pieces[0].shape[2]
    for r, ref in enumerate(pieces):
        at = info[1] ^ r
        there = pl.ds(pl.multiple_of((at * HALVES + half) * share, share), share)
        here = pl.ds(pl.multiple_of(at * share, share), share)
        for c in range(3):
            rhs[c, :, here] = velocity[c, :, there] - TIME_STEP * ref[c]
    nt = (((1,), (1,)), ((), ()))
    lanes = slice(half * rhs.shape[2], (half + 1) * rhs.shape[2])
    parts = []
    for c in range(3):
        high, low = split(rhs[c])
        total = lax.dot_general(high, fh[:, lanes], nt, preferred_element_type=F32)
        total += lax.dot_general(low, fh[:, lanes], nt, preferred_element_type=F32)
        total += lax.dot_general(high, fl[:, lanes], nt, preferred_element_type=F32)
        parts.append(total)
    return parts


def early_kernel(info, velocity, own, one, two, three, fh, fl, rhs, force):
    parts = lifted(0, info, velocity, (own, one, two, three), fh, fl, rhs)
    for c in range(3):
        force[c] = parts[c]


def forcing_kernel(info, velocity, own, one, two, three, fh, fl, before, rhs, f0, f1, f2, f3, force):
    place = info[0] % GROUP
    parts = lifted(1, info, velocity, (own, one, two, three), fh, fl, rhs)
    for c in range(3):
        force[c] = before[c] + parts[c]
    rows = f0.shape[0] // 3
    for r, ref in enumerate((f0, f1, f2, f3)):
        at = pl.ds(pl.multiple_of(((place + r) % GROUP) * rows, rows), rows)
        for c in range(3):
            ref[c * rows : (c + 1) * rows, :] = force[c, at, :]


def ends(first, last):
    return jnp.where(low_half(last), last, first)


def ahead(t, ah, al):
    first = product(t[0], ah[0, :, :EDGE], al[0, :, :EDGE])
    last = product(t[GROUP - 1], ah[GROUP - 1, :, :EDGE], al[GROUP - 1, :, :EDGE])
    return ends(first, last)


def advance(t, winv, keep, wf, ah, al, t_out):
    terms = [product(t[p], ah[p], al[p]) for p in range(GROUP)]
    for p, total in enumerate(assemble(terms)):
        t_out[p] = triple(keep[p]) * t[p] + wf[p] - triple(winv[p]) * total
    return terms


def start_kernel(info, f0, f1, f2, f3, winv, ah, al, wf, t_out, message, gather):
    place = info[0] % GROUP
    for r, ref in enumerate((f0, f1, f2, f3)):
        gather[(place + GROUP - r) % GROUP] = ref[...]
    terms = [gather[p] for p in range(GROUP)]
    message[:, :EDGE] = ends(terms[0][:, :EDGE], terms[GROUP - 1][:, :EDGE])
    for p, total in enumerate(assemble(terms)):
        now = triple(winv[p]) * total
        wf[p] = now
        t_out[p] = now
    message[:, EDGE:] = ahead(t_out, ah, al)


def inner_kernel(t, winv, keep, wf, ah, al, t_out):
    advance(t, winv, keep, wf, ah, al, t_out)


def correct(sign, t, message, left, right, winv, keep, ah, al, bh, bl):
    scale = sign * triple(ends(winv[0, :, :EDGE], winv[GROUP - 1, :, :EDGE]))
    hold = triple(ends(keep[0, :, :EDGE], keep[GROUP - 1, :, :EDGE]))
    share = scale * meet(left[:, :EDGE], right[:, :EDGE])
    theirs = scale * message[:, :EDGE]
    late = meet(left[:, EDGE:], right[:, EDGE:]) + product(theirs, bh[...], bl[...])
    low = low_half(share)
    share_last = jnp.where(low, share, 0.0)
    share_first = jnp.where(low, 0.0, share)
    none = jnp.zeros((share.shape[0], NODES), F32)
    terms = [none] * GROUP
    terms[0] = product(share_first, ah[0, :EDGE, :], al[0, :EDGE, :])
    terms[GROUP - 1] = product(share_last, ah[GROUP - 1, :EDGE, :], al[GROUP - 1, :EDGE, :])
    sums = assemble(terms)
    add = hold * share - sign * scale * late
    if sign > 0:
        add = add + share
    parts = [jnp.where(low, 0.0, add)] + [None] * (GROUP - 2) + [jnp.where(low, add, 0.0)]
    result = []
    for p in range(GROUP):
        now = t[p] - triple(winv[p]) * sums[p]
        if parts[p] is not None:
            now = jnp.concatenate([now[:, :EDGE] + parts[p], now[:, EDGE:]], axis=1)
        result.append(now)
    return result, share


def sweep_kernel(t, message, left, right, winv, keep, wf, ah, al, bh, bl, t_out, out_message, now):
    result, _ = correct(-1.0, t, message, left, right, winv, keep, ah, al, bh, bl)
    send_on(result, winv, keep, wf, ah, al, t_out, out_message, now)


def send_on(result, winv, keep, wf, ah, al, t_out, out_message, now):
    for p in range(GROUP):
        now[p] = result[p]
    terms = advance(now, winv, keep, wf, ah, al, t_out)
    out_message[:, :EDGE] = ends(terms[0][:, :EDGE], terms[GROUP - 1][:, :EDGE])
    out_message[:, EDGE:] = ahead(t_out, ah, al)


def second_kernel(t, message, left, right, winv, keep, wf, ah, al, bh, bl, t_out, out_message, wf_out, now):
    result, share = correct(1.0, t, message, left, right, winv, keep, ah, al, bh, bl)
    low = low_half(share)
    for p in range(GROUP):
        wf_out[p] = wf[p]
    wf_out[0, :, :EDGE] += jnp.where(low, 0.0, share)
    wf_out[GROUP - 1, :, :EDGE] += jnp.where(low, share, 0.0)
    send_on(result, winv, keep, wf_out, ah, al, t_out, out_message, now)


def last_kernel(info, t, message, left, right, winv, keep, ah, al, bh, bl, o0, o1, o2, o3, now):
    result, _ = correct(-1.0, t, message, left, right, winv, keep, ah, al, bh, bl)
    for p in range(GROUP):
        now[p] = result[p]
    place = info[0] % GROUP
    for r, ref in enumerate((o0, o1, o2, o3)):
        ref[...] = now[(place + r) % GROUP]


def final_kernel(info, pos, t0, t1, t2, t3, rhs0, rhs1, fh, fl, out_hbm, trace_hbm, t, turned, out, trace, sems):
    place = info[0] % GROUP
    modes, width = rhs0.shape[1:]
    rows = t0.shape[0] // 3
    share = width // 4
    for r, ref in enumerate((t0, t1, t2, t3)):
        at = pl.ds(pl.multiple_of(((place + GROUP - r) % GROUP) * rows, rows), rows)
        for c in range(3):
            t[c, at, :] = ref[c * rows : (c + 1) * rows, :]
    copies = []
    for c in range(3):
        high, low = split(t[c])
        both = dot(jnp.concatenate([high, low], axis=0), fh[...])
        both = both[:modes] + both[modes:] + dot(high, fl[...])
        for half, rhs in enumerate((rhs0, rhs1)):
            for q in range(4):
                lanes = slice((q * HALVES + half) * share, (q * HALVES + half + 1) * share)
                here = slice(q * share, (q + 1) * share)
                from_t = both[:, half * width + q * share : half * width + (q + 1) * share]
                out[c, :, lanes] = rhs[c, :, here] + from_t
        copies.append(pltpu.make_async_copy(out.at[c], out_hbm.at[c], sems.at[c]))
        copies[c].start()
        turned[:, c * modes : (c + 1) * modes] = t[c].T
    for face in range(trace.shape[0] // NODES1):
        row = pl.multiple_of(pos[face] * NODES1, NODES1)
        trace[face * NODES1 : (face + 1) * NODES1, :] = turned[pl.ds(row, NODES1), :]
    copies.append(pltpu.make_async_copy(trace, trace_hbm, sems.at[3]))
    copies[3].start()
    for copy in copies:
        copy.wait()


def call(kernel, outs, *args, smem=(), smem_out=(), hbm=(), hbm_out=(), scratch=(), flops=0, limit=32):
    size = sum(x.size * x.dtype.itemsize for x in (*args, *outs))
    return pl.pallas_call(
        kernel,
        out_shape=tuple(outs),
        in_specs=[SMEM if k in smem else HBM if k in hbm else VMEM for k in range(len(args))],
        out_specs=tuple(
            SMEM if k in smem_out else HBM if k in hbm_out else VMEM for k in range(len(outs))
        ),
        scratch_shapes=list(scratch),
        cost_estimate=pl.CostEstimate(flops=int(flops), bytes_accessed=int(size), transcendentals=0),
        compiler_params=pltpu.CompilerParams(vmem_limit_bytes=limit * 2**20),
    )(*args)


def arr(*shape, dtype=F32):
    return jax.ShapeDtypeStruct(shape, dtype)


def shards(velocity, metric, lift, blocks, conn, send_list):
    modes, points = velocity.shape[1:]
    ways = lax.axis_size("mode")
    planes = modes * ways
    share = points // ways
    elem_count, width = lift.shape[:2]
    faces = 2 * elem_count
    half = EDGE // 2
    rows = 3 * modes // GROUP
    me = lax.axis_index("mode")
    part = lax.axis_index("elem")
    count = lax.axis_size("elem")
    info = jnp.stack([part, me]).astype(jnp.int32)

    def swap(x, r):
        return lax.ppermute(x, "mode", [(j, j ^ r) for j in range(ways)])

    def turn(x, r):
        pairs = [(i, i - i % GROUP + (i + r) % GROUP) for i in range(count)]
        return lax.ppermute(x, "elem", pairs)

    def exchange(x):
        left = lax.ppermute(x, "elem", [(i, (i + GROUP) % count) for i in range(count)])
        right = lax.ppermute(x, "elem", [((i + GROUP) % count, i) for i in range(count)])
        return left, right

    size = share // HALVES
    chunk = arr(3, modes, size)

    def cut(r, h):
        return lax.dynamic_slice_in_dim(velocity, ((me ^ r) * HALVES + h) * size, size, 2)

    got = [{r: cut(r, h) for r in range(ways)} for h in range(HALVES)]
    for h in range(HALVES):
        for r in (2, 3):
            if h == 1 and r == 3:
                mine = (got[1][3], got[0][2], got[0][3])
                got[1][3], got[0][2], got[0][3] = lax.optimization_barrier(mine)
            got[h][r] = swap(got[h][r], r)
    got[0][1] = swap(got[0][1], 1)

    (packed,) = call(
        pack_kernel,
        [arr(elem_count * NODES1 + NODES1, 4 * width)],
        conn, send_list, blocks,
        smem=(0, 1),
        limit=4,
    )
    fh, fl, pos = call(
        lift_kernel,
        [
            arr(NODES, points, dtype=BF16),
            arr(NODES, points, dtype=BF16),
            arr(faces, dtype=jnp.int32),
        ],
        info, conn, send_list, lift,
        smem=(0, 1, 2),
        smem_out=(2,),
        scratch=[pltpu.VMEM((NODES, points), F32)],
        flops=2e9,
        limit=8,
    )
    packed, got[0][1] = lax.optimization_barrier((packed, got[0][1]))
    fh, got[0][1] = lax.optimization_barrier((fh, got[0][1]))
    packs = jnp.stack([packed] + [turn(packed, GROUP - r) for r in range(1, GROUP)])
    packs, theirs = lax.optimization_barrier((packs, got[1][1]))
    got[1][1] = swap(theirs, 1)
    ints = packs[:, -NODES1, :].astype(jnp.int32).reshape(-1)
    tables = [jnp.asarray(x) for x in (*plane_tables(planes), *node_table(size))]
    tables = call(
        fetch_kernel,
        [
            arr(2 * planes, 3 * planes, dtype=BF16),
            arr(planes, 3 * planes, dtype=BF16),
            arr(3 * size, 2 * size, dtype=BF16),
        ],
        *tables,
        hbm=tuple(range(6)),
        scratch=[pltpu.SemaphoreType.DMA((9,))],
        limit=4,
    )
    home = []
    for h in range(HALVES):
        outs = call(
            functools.partial(advect_kernel, h),
            [chunk] * 4,
            info,
            *(got[h][r] for r in range(4)),
            metric,
            *tables,
            smem=(0,),
            scratch=[pltpu.VMEM((3 * planes, 3 * share // HALVES), BF16)] * 2,
            flops=4e9,
            limit=12,
        )
        home.append({0: outs[0]})
        for r in (2, 3, 1):
            home[h][r] = swap(outs[r], r)
        if h == 0:
            continue
        packs, home[h][0] = lax.optimization_barrier((packs, home[h][0]))
        ah, al, dgp, tie = call(
            setup_kernel,
            [
                arr(GROUP, NODES, NODES, dtype=BF16),
                arr(GROUP, NODES, NODES, dtype=BF16),
                arr(GROUP, NODES1, NODES),
                arr(half + NODES1, EDGE),
            ],
            info, ints, packs,
            smem=(0, 1),
            scratch=[
                pltpu.SMEM((faces,), jnp.int32),
                pltpu.VMEM((NODES, NODES), F32),
                pltpu.VMEM((NODES, 128), F32),
            ],
            flops=8e9,
            limit=10,
        )
    piece = arr(rows, NODES)
    rhs_part = arr(3, modes, points // HALVES)
    home[0][0], home[1][0] = lax.optimization_barrier((home[0][0], home[1][0]))
    rhs0, early = call(
        early_kernel,
        [rhs_part, arr(3, modes, NODES)],
        info, velocity, *(home[0][r] for r in range(4)), fh, fl,
        smem=(0,),
        flops=1.7e9,
        limit=10,
    )
    early, tie = lax.optimization_barrier((early, tie))
    rhs1, *force = call(
        forcing_kernel,
        [rhs_part] + [piece] * GROUP,
        info, velocity, *(home[1][r] for r in range(4)), fh, fl, early,
        smem=(0,),
        scratch=[pltpu.VMEM((3, modes, NODES), F32)],
        flops=1.7e9,
        limit=10,
    )
    moved = {r: turn(force[r], r) for r in (2, 1, 3)}
    tie, force[0] = lax.optimization_barrier((tie, force[0]))
    tie_left, tie_right = exchange(tie)
    winv, keep, bh, bl = call(
        weights_kernel,
        [arr(GROUP, rows // 3, NODES)] * 2 + [arr(EDGE, EDGE, dtype=BF16)] * 2,
        info, dgp, tie_left, tie_right,
        smem=(0,),
        limit=8,
    )

    state = arr(GROUP, rows, NODES)
    note = arr(rows, 2 * EDGE)
    scratch = [pltpu.VMEM((GROUP, rows, NODES), F32)]
    wf, t, message = call(
        start_kernel,
        [state, state, note],
        info, force[0], moved[1], moved[2], moved[3], winv, ah, al,
        smem=(0,),
        scratch=scratch,
        flops=1e8,
        limit=8,
    )
    for pair in range(SWEEPS // 2):
        left, right = exchange(message)
        (t,) = call(inner_kernel, [state], t, winv, keep, wf, ah, al, flops=3e8, limit=8)
        if pair == SWEEPS // 2 - 1:
            break
        args = (t, message, left, right, winv, keep, wf, ah, al, bh, bl)
        if pair == 0:
            t, message, wf = call(
                second_kernel, [state, note, state], *args, scratch=scratch, flops=4e8, limit=8
            )
        else:
            t, message = call(sweep_kernel, [state, note], *args, scratch=scratch, flops=4e8, limit=8)
    ends_out = call(
        last_kernel,
        [piece] * GROUP,
        info, t, message, left, right, winv, keep, ah, al, bh, bl,
        smem=(0,),
        scratch=scratch,
        flops=1e8,
        limit=8,
    )
    there = {r: turn(ends_out[r], r) for r in (2, 1, 3)}
    velocity_new, trace = call(
        final_kernel,
        [arr(3, modes, points), arr(faces * NODES1, 3 * modes)],
        info, pos, ends_out[0], there[1], there[2], there[3], rhs0, rhs1, fh, fl,
        smem=(0, 1),
        hbm_out=(0, 1),
        scratch=[
            pltpu.VMEM((3, modes, NODES), F32),
            pltpu.VMEM((NODES, 3 * modes), F32),
            pltpu.VMEM((3, modes, points), F32),
            pltpu.VMEM((faces * NODES1, 3 * modes), F32),
            pltpu.SemaphoreType.DMA((4,)),
        ],
        flops=1e9,
        limit=10,
    )
    return velocity_new, trace.reshape(faces, NODES1, 3, modes)


def solution(mesh):
    return jax.shard_map(
        shards,
        mesh=mesh,
        in_specs=(
            P(None, "mode", "elem"),
            P(None, "elem"),
            P("elem", None, None),
            P("elem", None, None),
            P("elem", None),
            P("elem", None),
        ),
        out_specs=(P(None, "mode", "elem"), P("elem", None, None, "mode")),
        check_vma=False,
    )
```

```python
import functools
import math

import jax
import jax.numpy as jnp
import ml_dtypes
import numpy as np
from jax import lax
from jax.experimental import pallas as pl
from jax.experimental.pallas import tpu as pltpu
from jax.sharding import PartitionSpec as P

NODES1 = 8
SWEEPS = 8
PLANES = 512
GROUP = 4
EDGE = 128
HALVES = 2
NODES = 384
TIME_STEP = 0.01
RELAXATION = 0.8
HELMHOLTZ_BASE = 0.5
F32 = jnp.float32
BF16 = jnp.bfloat16
VMEM = pl.BlockSpec(memory_space=pltpu.VMEM)
HBM = pl.BlockSpec(memory_space=pltpu.HBM)
SMEM = pl.BlockSpec(memory_space=pltpu.SMEM)


def split(x):
    high = x.astype(BF16)
    return high, (x - high.astype(F32)).astype(BF16)


def dot(a, b):
    return jnp.dot(a, b, preferred_element_type=F32)


def np_split(x):
    high = x.astype(np.float32).astype(ml_dtypes.bfloat16)
    low = (x - high.astype(np.float64)).astype(np.float32).astype(ml_dtypes.bfloat16)
    return high, low


def edge_derivative(length):
    index = np.arange(length)
    points_at = np.cos(math.pi * index / (length - 1))
    weights = np.where((index == 0) | (index == length - 1), 2.0, 1.0)
    signs = 1.0 - 2.0 * ((index[:, None] + index[None, :]) % 2)
    same = index[:, None] == index[None, :]
    spacing = np.where(same, 1.0, points_at[:, None] - points_at[None, :])
    offdiag = np.where(same, 0.0, weights[:, None] / weights[None, :] * signs / spacing)
    return offdiag - np.diag(offdiag.sum(axis=1))


def node_table(share):
    edge = edge_derivative(NODES1)
    eye = np.eye(NODES1)
    several = np.eye(share // (NODES1 * NODES1))
    along_r = np.kron(several, np.kron(eye, edge)).T
    along_s = np.kron(several, np.kron(edge, eye)).T
    return np_split(np.concatenate([along_r, along_s], axis=1))


def plane_tables(length):
    plane = np.arange(length)[:, None]
    column = np.arange(length)[None, :]
    wave = (column + 1) // 2
    angle = 2.0 * math.pi / length * (wave * plane % length)
    is_sine = (column % 2 == 0) & (column > 0)
    is_edge = (column == 0) | (column == length - 1)
    factor = np.where(is_edge, math.sqrt(1.0 / length), math.sqrt(2.0 / length))
    rate = wave * (8.0 / length)
    basis = factor * np.where(is_sine, np.sin(angle), np.cos(angle))
    slope = factor * rate * np.where(is_sine, np.cos(angle), -np.sin(angle))
    slope = np.where(column == length - 1, 0.0, slope)
    return (*np_split(np.concatenate([basis, slope], axis=0)), *np_split(basis.T))


def pack_kernel(conn, send, blocks, out):
    elem_count, width = blocks.shape[:2]
    for e in range(elem_count):
        parts = [blocks[e, NODES1 * j : NODES1 * (j + 1), :] for j in range(4)]
        out[NODES1 * e : NODES1 * (e + 1), :] = jnp.concatenate(parts, axis=1)
    lane = lax.broadcasted_iota(jnp.int32, (NODES1, 4 * width), 1)
    row = jnp.zeros_like(lane)
    numbers = [conn[e, j] for e in range(elem_count) for j in range(4)]
    numbers += [send[0, k] for k in range(send.shape[1])]
    for k, number in enumerate(numbers):
        row = jnp.where(lane == k, number, row)
    out[NODES1 * elem_count :, :] = row.astype(F32)


def lift_kernel(info, conn, send, lift, fh, fl, pos, f):
    elem_count, _, node_count = lift.shape
    faces = 2 * elem_count
    halo = send.shape[1]
    for face in range(faces):
        pos[face] = jnp.int32(-1)
    for k in range(halo):
        pos[send[0, k]] = jnp.int32(k)
    count = jnp.int32(2 * halo)
    for face in range(faces):
        now = pos[face]
        pos[face] = jnp.where(now < 0, count, now)
        count = count + jnp.where(now < 0, 1, 0)
    f[...] = jnp.zeros_like(f)
    quarter = elem_count // 4
    piece = quarter // HALVES
    for e in range(elem_count):
        q, rest = divmod(e, quarter)
        half, rest = divmod(rest, piece)
        column = ((half * 4 + q) * piece + rest) * node_count
        nodes = slice(column, column + node_count)
        for j in range(4):
            slot = conn[e, j]
            own = slot < faces
            at = jnp.where(own, pos[jnp.minimum(slot, faces - 1)], slot - (faces - halo))
            live = jnp.where(own | (info[0] > 0), 1.0, 0.0).astype(F32)
            here = pl.ds(pl.multiple_of(NODES1 * at, NODES1), NODES1)
            part = slice(NODES1 * j, NODES1 * (j + 1))
            f[here, nodes] += live * lift[e, part, :]
    high, low = split(f[...])
    fh[...] = high
    fl[...] = low


def setup_kernel(info, ints, packs, ah, al, dgp, tie, pos, a, dg):
    width = packs.shape[2] // 4
    elem_count = packs.shape[1] // NODES1 - 1
    faces = 2 * elem_count
    halo = faces // 4
    place = info[0] % GROUP
    lane = lax.broadcasted_iota(jnp.int32, (NODES1, NODES), 1)
    sub = lax.broadcasted_iota(jnp.int32, (NODES1, NODES), 0)
    diagonal = lax.broadcasted_iota(jnp.int32, (NODES1, width), 1)
    row_of = lax.broadcasted_iota(jnp.int32, (NODES1, width), 0)
    first_half = lax.broadcasted_iota(jnp.int32, (NODES1, 128), 1) < 64

    def one(step, carry):
        r = GROUP - 1 - step
        p = (place + r) % GROUP
        whole = (info[0] - place + p) > 0
        base = r * 128
        for face in range(faces):
            pos[face] = jnp.int32(-1)
        for k in range(halo):
            pos[ints[base + 4 * elem_count + k]] = jnp.int32(k)
        count = jnp.int32(2 * halo)
        for face in range(faces):
            now = pos[face]
            pos[face] = jnp.where(now < 0, count, now)
            count = count + jnp.where(now < 0, 1, 0)
        a[...] = jnp.zeros_like(a)
        dg[...] = jnp.zeros_like(dg)
        for e in range(elem_count):
            at, live = [], []
            for j in range(4):
                slot = ints[base + 4 * e + j]
                own = slot < faces
                at.append(jnp.where(own, pos[jnp.minimum(slot, faces - 1)], slot - (faces - halo)))
                live.append(jnp.where(own | whole, 1.0, 0.0).astype(F32))
            spread = jnp.concatenate(
                [jnp.where(lane == sub + NODES1 * at[j], live[j], 0.0) for j in range(4)], axis=0
            )
            packed = packs[r, NODES1 * e : NODES1 * (e + 1), :]
            block = jnp.concatenate([packed[:, width * j : width * (j + 1)] for j in range(4)], axis=0)
            rows = jnp.dot(block, spread, precision=lax.Precision.HIGHEST, preferred_element_type=F32)
            for j in range(4):
                here = pl.ds(pl.multiple_of(NODES1 * at[j], NODES1), NODES1)
                part = slice(NODES1 * j, NODES1 * (j + 1))
                own_rows = block[part]
                diag = jnp.sum(
                    jnp.where(diagonal == row_of + NODES1 * j, own_rows, 0.0), axis=1, keepdims=True
                )
                diag = jnp.where(first_half, jnp.broadcast_to(diag, (NODES1, 128)), 1.0)
                a[here, :] += live[j] * rows[part]
                dg[here, :] += live[j] * diag

        high, low = split(a[...].T)
        ah[p] = high
        al[p] = low
        turned = dg[...].T
        dgp[p, 0:1, :] = turned[0:1]
        dgp[p, 1:2, :] = turned[64:65]
        return carry

    lax.fori_loop(0, GROUP, one, 0)
    half = halo * NODES1
    last = ah[GROUP - 1, :half, :EDGE].astype(F32) + al[GROUP - 1, :half, :EDGE].astype(F32)
    first = ah[0, half:EDGE, :EDGE].astype(F32) + al[0, half:EDGE, :EDGE].astype(F32)
    tie[:half, :] = jnp.where(low_half(last), last, first)
    tie[half : half + NODES1, :] = jnp.where(
        low_half(dgp[0, :, :EDGE]), dgp[GROUP - 1, :, :EDGE], dgp[0, :, :EDGE]
    )


def low_half(x):
    return lax.broadcasted_iota(jnp.int32, x.shape, x.ndim - 1) < EDGE // 2


def meet(left, right):
    return pltpu.roll(jnp.where(low_half(left), left, right), EDGE // 2, 1)


def triple(x):
    return jnp.concatenate([x, x, x], axis=0)


def assemble(terms, before=None, after=None):
    zero = jnp.zeros_like(terms[0][:, :EDGE])
    sums = []
    for p, term in enumerate(terms):
        left = terms[p - 1][:, :EDGE] if p > 0 else (zero if before is None else before)
        right = terms[p + 1][:, :EDGE] if p < GROUP - 1 else (zero if after is None else after)
        sums.append(jnp.concatenate([term[:, :EDGE] + meet(left, right), term[:, EDGE:]], axis=1))
    return sums


def weights_kernel(info, dgp, tie_left, tie_right, winv, keep, bh, bl):
    half = EDGE // 2
    rows = winv.shape[1]
    base = info[1] * (rows * GROUP) + (info[0] % GROUP) * rows
    wave = (lax.broadcasted_iota(jnp.int32, (rows, 1), 0) + base + 1) // 2
    rate = wave.astype(F32) * (8.0 / PLANES)
    kappa = HELMHOLTZ_BASE + rate * rate
    sums = assemble([dgp[p] for p in range(GROUP)], tie_left[half:, :], tie_right[half:, :])
    for p in range(GROUP):
        diag = sums[p][0:1]
        hits = kappa * sums[p][1:2]
        diag = jnp.where(sums[p][1:2] > 0.0, diag, 1.0)
        inverse = RELAXATION / (diag + hits)
        winv[p] = inverse
        keep[p] = 1.0 - inverse * hits
    right = pltpu.roll(tie_right[:half, :], half, 1)
    left = pltpu.roll(tie_left[:half, :], half, 1)
    corner = jnp.concatenate(
        [jnp.where(low_half(right), right, 0.0), jnp.where(low_half(left), 0.0, left)], axis=0
    )
    high, low = split(corner)
    bh[...] = high
    bl[...] = low


def fetch_kernel(forward_high, forward_low, back_high, back_low, high, low, forward, back, nodes, sems):
    copies = []
    for first, second, out in ((forward_high, forward_low, forward), (back_high, back_low, back)):
        size = first.shape[1]
        for k, table in enumerate((first, first, second)):
            there = out.at[:, k * size : (k + 1) * size]
            copies.append(pltpu.make_async_copy(table, there, sems.at[len(copies)]))
    size = high.shape[0]
    for k, table in enumerate((high, high, low)):
        there = nodes.at[k * size : (k + 1) * size, :]
        copies.append(pltpu.make_async_copy(table, there, sems.at[len(copies)]))
    for copy in copies:
        copy.start()
    for copy in copies:
        copy.wait()


def advect_kernel(half, info, own, one, two, three, metric, forward, back, nodes, o0, o1, o2, o3, c3, n3):
    me = info[1]
    modes, share = own.shape[1], own.shape[2]
    planes = back.shape[0]
    for r, ref in enumerate((own, one, two, three)):
        row = pl.multiple_of((me ^ r) * modes, modes)
        for c in range(3):
            high, low = split(ref[c])
            lanes = slice(c * share, (c + 1) * share)
            c3[pl.ds(row, modes), lanes] = high
            c3[pl.ds(planes + row, modes), lanes] = low
            c3[pl.ds(2 * planes + row, modes), lanes] = high
    here = metric[:, pl.ds(pl.multiple_of((me * HALVES + half) * share, share), share)]
    rx, sx, ry, sy = (here[k : k + 1, :] for k in range(4))
    step = 128
    for start in range(0, planes, step):
        rows = slice(start, start + step)
        physical = dot(forward[rows, :], c3[...])
        along_z = dot(forward[planes + start : planes + start + step, :], c3[...])
        stacked = jnp.concatenate(
            [physical[:, c * share : (c + 1) * share] for c in range(3)], axis=0
        )
        high, low = split(stacked)
        slopes = dot(jnp.concatenate([high, low, high], axis=1), nodes[...])
        p0, p1, p2 = (physical[:, c * share : (c + 1) * share] for c in range(3))
        for c in range(3):
            lanes = slice(c * share, (c + 1) * share)
            by_r = slopes[c * step : (c + 1) * step, :share]
            by_s = slopes[c * step : (c + 1) * step, share:]
            term = p0 * (rx * by_r + sx * by_s) + p1 * (ry * by_r + sy * by_s)
            term = term + p2 * along_z[:, lanes]
            high, low = split(term)
            n3[start : start + step, lanes] = high
            n3[planes + start : planes + start + step, lanes] = low
            n3[2 * planes + start : 2 * planes + start + step, lanes] = high
    for r, ref in ((2, o2), (3, o3), (1, o1), (0, o0)):
        row = pl.multiple_of((me ^ r) * modes, modes)
        spectral = dot(back[pl.ds(row, modes), :], n3[...])
        for c in range(3):
            ref[c] = spectral[:, c * share : (c + 1) * share]


def product(t, high_table, low_table):
    rows = t.shape[0]
    high, low = split(t)
    both = dot(jnp.concatenate([high, low], axis=0), high_table)
    return both[:rows] + both[rows:] + dot(high, low_table)


def lifted(half, info, velocity, pieces, fh, fl, rhs):
    share = pieces[0].shape[2]
    for r, ref in enumerate(pieces):
        at = info[1] ^ r
        there = pl.ds(pl.multiple_of((at * HALVES + half) * share, share), share)
        here = pl.ds(pl.multiple_of(at * share, share), share)
        for c in range(3):
            rhs[c, :, here] = velocity[c, :, there] - TIME_STEP * ref[c]
    nt = (((1,), (1,)), ((), ()))
    lanes = slice(half * rhs.shape[2], (half + 1) * rhs.shape[2])
    parts = []
    for c in range(3):
        high, low = split(rhs[c])
        total = lax.dot_general(high, fh[:, lanes], nt, preferred_element_type=F32)
        total += lax.dot_general(low, fh[:, lanes], nt, preferred_element_type=F32)
        total += lax.dot_general(high, fl[:, lanes], nt, preferred_element_type=F32)
        parts.append(total)
    return parts


def early_kernel(info, velocity, own, one, two, three, fh, fl, rhs, force):
    parts = lifted(0, info, velocity, (own, one, two, three), fh, fl, rhs)
    for c in range(3):
        force[c] = parts[c]


def forcing_kernel(info, velocity, own, one, two, three, fh, fl, before, rhs, f0, f1, f2, f3, force):
    place = info[0] % GROUP
    parts = lifted(1, info, velocity, (own, one, two, three), fh, fl, rhs)
    for c in range(3):
        force[c] = before[c] + parts[c]
    rows = force.shape[1] // GROUP
    for r, ref in enumerate((f0, f1, f2, f3)):
        at = pl.ds(pl.multiple_of(((place + r) % GROUP) * rows, rows), rows)
        ref[...] = fold(jnp.concatenate([force[c, at, :] for c in range(3)], axis=0))


def fold(x):
    rows = x.shape[0]
    rest = [x[k * rows // 4 : (k + 1) * rows // 4, 256:320] for k in range(4)]
    return jnp.concatenate([x[:, :256], jnp.concatenate(rest, axis=1)], axis=0)


def unfold(x):
    rows = x.shape[0] * 4 // 5
    rest = jnp.concatenate([x[rows:, 64 * k : 64 * (k + 1)] for k in range(4)], axis=0)
    return jnp.concatenate([x[:rows], rest, jnp.zeros_like(rest)], axis=1)


def ends(first, last):
    return jnp.where(low_half(last), last, first)


def ahead(t, ah, al):
    first = product(t[0], ah[0, :, :EDGE], al[0, :, :EDGE])
    last = product(t[GROUP - 1], ah[GROUP - 1, :, :EDGE], al[GROUP - 1, :, :EDGE])
    return ends(first, last)


def advance(t, winv, keep, wf, ah, al, t_out):
    terms = [product(t[p], ah[p], al[p]) for p in range(GROUP)]
    for p, total in enumerate(assemble(terms)):
        t_out[p] = triple(keep[p]) * t[p] + wf[p] - triple(winv[p]) * total
    return terms


def start_kernel(info, f0, f1, f2, f3, winv, ah, al, wf, t_out, message, gather):
    place = info[0] % GROUP
    for r, ref in enumerate((f0, f1, f2, f3)):
        gather[(place + GROUP - r) % GROUP] = unfold(ref[...])
    terms = [gather[p] for p in range(GROUP)]
    message[:, :EDGE] = ends(terms[0][:, :EDGE], terms[GROUP - 1][:, :EDGE])
    for p, total in enumerate(assemble(terms)):
        now = triple(winv[p]) * total
        wf[p] = now
        t_out[p] = now
    message[:, EDGE:] = ahead(t_out, ah, al)


def inner_kernel(t, winv, keep, wf, ah, al, t_out):
    advance(t, winv, keep, wf, ah, al, t_out)


def correct(sign, t, message, left, right, winv, keep, ah, al, bh, bl):
    scale = sign * triple(ends(winv[0, :, :EDGE], winv[GROUP - 1, :, :EDGE]))
    hold = triple(ends(keep[0, :, :EDGE], keep[GROUP - 1, :, :EDGE]))
    share = scale * meet(left[:, :EDGE], right[:, :EDGE])
    theirs = scale * message[:, :EDGE]
    late = meet(left[:, EDGE:], right[:, EDGE:]) + product(theirs, bh[...], bl[...])
    low = low_half(share)
    share_last = jnp.where(low, share, 0.0)
    share_first = jnp.where(low, 0.0, share)
    none = jnp.zeros((share.shape[0], NODES), F32)
    terms = [none] * GROUP
    terms[0] = product(share_first, ah[0, :EDGE, :], al[0, :EDGE, :])
    terms[GROUP - 1] = product(share_last, ah[GROUP - 1, :EDGE, :], al[GROUP - 1, :EDGE, :])
    sums = assemble(terms)
    add = hold * share - sign * scale * late
    if sign > 0:
        add = add + share
    parts = [jnp.where(low, 0.0, add)] + [None] * (GROUP - 2) + [jnp.where(low, add, 0.0)]
    result = []
    for p in range(GROUP):
        now = t[p] - triple(winv[p]) * sums[p]
        if parts[p] is not None:
            now = jnp.concatenate([now[:, :EDGE] + parts[p], now[:, EDGE:]], axis=1)
        result.append(now)
    return result, share


def sweep_kernel(t, message, left, right, winv, keep, wf, ah, al, bh, bl, t_out, out_message, now):
    result, _ = correct(-1.0, t, message, left, right, winv, keep, ah, al, bh, bl)
    send_on(result, winv, keep, wf, ah, al, t_out, out_message, now)


def send_on(result, winv, keep, wf, ah, al, t_out, out_message, now):
    for p in range(GROUP):
        now[p] = result[p]
    terms = advance(now, winv, keep, wf, ah, al, t_out)
    out_message[:, :EDGE] = ends(terms[0][:, :EDGE], terms[GROUP - 1][:, :EDGE])
    out_message[:, EDGE:] = ahead(t_out, ah, al)


def second_kernel(t, message, left, right, winv, keep, wf, ah, al, bh, bl, t_out, out_message, wf_out, now):
    result, share = correct(1.0, t, message, left, right, winv, keep, ah, al, bh, bl)
    low = low_half(share)
    for p in range(GROUP):
        wf_out[p] = wf[p]
    wf_out[0, :, :EDGE] += jnp.where(low, 0.0, share)
    wf_out[GROUP - 1, :, :EDGE] += jnp.where(low, share, 0.0)
    send_on(result, winv, keep, wf_out, ah, al, t_out, out_message, now)


def last_kernel(info, t, message, left, right, winv, keep, ah, al, bh, bl, o0, o1, o2, o3, now):
    result, _ = correct(-1.0, t, message, left, right, winv, keep, ah, al, bh, bl)
    for p in range(GROUP):
        now[p] = result[p]
    place = info[0] % GROUP
    for r, ref in enumerate((o0, o1, o2, o3)):
        ref[...] = fold(now[(place + r) % GROUP])


def final_kernel(info, pos, t0, t1, t2, t3, rhs0, rhs1, fh, fl, out_hbm, trace_hbm, t, turned, out, trace, sems):
    place = info[0] % GROUP
    modes, width = rhs0.shape[1:]
    rows = modes // GROUP
    share = width // 4
    for r, ref in enumerate((t0, t1, t2, t3)):
        at = pl.ds(pl.multiple_of(((place + GROUP - r) % GROUP) * rows, rows), rows)
        whole = unfold(ref[...])
        for c in range(3):
            t[c, at, :] = whole[c * rows : (c + 1) * rows, :]
    copies = []
    for c in range(3):
        high, low = split(t[c])
        both = dot(jnp.concatenate([high, low], axis=0), fh[...])
        both = both[:modes] + both[modes:] + dot(high, fl[...])
        for half, rhs in enumerate((rhs0, rhs1)):
            for q in range(4):
                lanes = slice((q * HALVES + half) * share, (q * HALVES + half + 1) * share)
                here = slice(q * share, (q + 1) * share)
                from_t = both[:, half * width + q * share : half * width + (q + 1) * share]
                out[c, :, lanes] = rhs[c, :, here] + from_t
        copies.append(pltpu.make_async_copy(out.at[c], out_hbm.at[c], sems.at[c]))
        copies[c].start()
        turned[:, c * modes : (c + 1) * modes] = t[c].T
    for face in range(trace.shape[0] // NODES1):
        row = pl.multiple_of(pos[face] * NODES1, NODES1)
        trace[face * NODES1 : (face + 1) * NODES1, :] = turned[pl.ds(row, NODES1), :]
    copies.append(pltpu.make_async_copy(trace, trace_hbm, sems.at[3]))
    copies[3].start()
    for copy in copies:
        copy.wait()


def call(kernel, outs, *args, smem=(), smem_out=(), hbm=(), hbm_out=(), scratch=(), flops=0, limit=32):
    size = sum(x.size * x.dtype.itemsize for x in (*args, *outs))
    return pl.pallas_call(
        kernel,
        out_shape=tuple(outs),
        in_specs=[SMEM if k in smem else HBM if k in hbm else VMEM for k in range(len(args))],
        out_specs=tuple(
            SMEM if k in smem_out else HBM if k in hbm_out else VMEM for k in range(len(outs))
        ),
        scratch_shapes=list(scratch),
        cost_estimate=pl.CostEstimate(flops=int(flops), bytes_accessed=int(size), transcendentals=0),
        compiler_params=pltpu.CompilerParams(vmem_limit_bytes=limit * 2**20),
    )(*args)


def arr(*shape, dtype=F32):
    return jax.ShapeDtypeStruct(shape, dtype)


def shards(velocity, metric, lift, blocks, conn, send_list):
    modes, points = velocity.shape[1:]
    ways = lax.axis_size("mode")
    planes = modes * ways
    share = points // ways
    elem_count, width = lift.shape[:2]
    faces = 2 * elem_count
    half = EDGE // 2
    rows = 3 * modes // GROUP
    me = lax.axis_index("mode")
    part = lax.axis_index("elem")
    count = lax.axis_size("elem")
    info = jnp.stack([part, me]).astype(jnp.int32)

    def swap(x, r):
        return lax.ppermute(x, "mode", [(j, j ^ r) for j in range(ways)])

    def turn(x, r):
        pairs = [(i, i - i % GROUP + (i + r) % GROUP) for i in range(count)]
        return lax.ppermute(x, "elem", pairs)

    def exchange(x):
        left = lax.ppermute(x, "elem", [(i, (i + GROUP) % count) for i in range(count)])
        right = lax.ppermute(x, "elem", [((i + GROUP) % count, i) for i in range(count)])
        return left, right

    size = share // HALVES
    chunk = arr(3, modes, size)

    def cut(r, h):
        return lax.dynamic_slice_in_dim(velocity, ((me ^ r) * HALVES + h) * size, size, 2)

    got = [{r: cut(r, h) for r in range(ways)} for h in range(HALVES)]
    for h in range(HALVES):
        for r in (2, 3):
            if h == 1 and r == 3:
                got[1][3], got[0][2] = lax.optimization_barrier((got[1][3], got[0][2]))
            got[h][r] = swap(got[h][r], r)
    got[0][1] = swap(got[0][1], 1)

    (packed,) = call(
        pack_kernel,
        [arr(elem_count * NODES1 + NODES1, 4 * width)],
        conn, send_list, blocks,
        smem=(0, 1),
        limit=4,
    )
    fh, fl, pos = call(
        lift_kernel,
        [
            arr(NODES, points, dtype=BF16),
            arr(NODES, points, dtype=BF16),
            arr(faces, dtype=jnp.int32),
        ],
        info, conn, send_list, lift,
        smem=(0, 1, 2),
        smem_out=(2,),
        scratch=[pltpu.VMEM((NODES, points), F32)],
        flops=2e9,
        limit=8,
    )
    packed, got[0][1] = lax.optimization_barrier((packed, got[0][1]))
    fh, got[0][1] = lax.optimization_barrier((fh, got[0][1]))
    packs = jnp.stack([packed] + [turn(packed, GROUP - r) for r in range(1, GROUP)])
    packs, theirs = lax.optimization_barrier((packs, got[1][1]))
    got[1][1] = swap(theirs, 1)
    ints = packs[:, -NODES1, :].astype(jnp.int32).reshape(-1)
    tables = [jnp.asarray(x) for x in (*plane_tables(planes), *node_table(size))]
    tables = call(
        fetch_kernel,
        [
            arr(2 * planes, 3 * planes, dtype=BF16),
            arr(planes, 3 * planes, dtype=BF16),
            arr(3 * size, 2 * size, dtype=BF16),
        ],
        *tables,
        hbm=tuple(range(6)),
        scratch=[pltpu.SemaphoreType.DMA((9,))],
        limit=4,
    )
    home = []
    for h in range(HALVES):
        outs = call(
            functools.partial(advect_kernel, h),
            [chunk] * 4,
            info,
            *(got[h][r] for r in range(4)),
            metric,
            *tables,
            smem=(0,),
            scratch=[pltpu.VMEM((3 * planes, 3 * share // HALVES), BF16)] * 2,
            flops=4e9,
            limit=8,
        )
        home.append({0: outs[0]})
        for r in (2, 3, 1):
            home[h][r] = swap(outs[r], r)
        if h == 0:
            continue
        packs, home[h][0] = lax.optimization_barrier((packs, home[h][0]))
        ah, al, dgp, tie = call(
            setup_kernel,
            [
                arr(GROUP, NODES, NODES, dtype=BF16),
                arr(GROUP, NODES, NODES, dtype=BF16),
                arr(GROUP, NODES1, NODES),
                arr(half + NODES1, EDGE),
            ],
            info, ints, packs,
            smem=(0, 1),
            scratch=[
                pltpu.SMEM((faces,), jnp.int32),
                pltpu.VMEM((NODES, NODES), F32),
                pltpu.VMEM((NODES, 128), F32),
            ],
            flops=8e9,
            limit=7,
        )
    piece = arr(rows * 5 // 4, 256)
    rhs_part = arr(3, modes, points // HALVES)
    home[0][0], home[1][0] = lax.optimization_barrier((home[0][0], home[1][0]))
    rhs0, early = call(
        early_kernel,
        [rhs_part, arr(3, modes, NODES)],
        info, velocity, *(home[0][r] for r in range(4)), fh, fl,
        smem=(0,),
        flops=1.7e9,
        limit=7,
    )
    early, tie = lax.optimization_barrier((early, tie))
    rhs1, *force = call(
        forcing_kernel,
        [rhs_part] + [piece] * GROUP,
        info, velocity, *(home[1][r] for r in range(4)), fh, fl, early,
        smem=(0,),
        scratch=[pltpu.VMEM((3, modes, NODES), F32)],
        flops=1.7e9,
        limit=7,
    )
    moved = {r: turn(force[r], r) for r in (2, 1, 3)}
    tie, force[0] = lax.optimization_barrier((tie, force[0]))
    tie_left, tie_right = exchange(tie)
    winv, keep, bh, bl = call(
        weights_kernel,
        [arr(GROUP, rows // 3, NODES)] * 2 + [arr(EDGE, EDGE, dtype=BF16)] * 2,
        info, dgp, tie_left, tie_right,
        smem=(0,),
        limit=8,
    )

    state = arr(GROUP, rows, NODES)
    note = arr(rows, 2 * EDGE)
    scratch = [pltpu.VMEM((GROUP, rows, NODES), F32)]
    wf, t, message = call(
        start_kernel,
        [state, state, note],
        info, force[0], moved[1], moved[2], moved[3], winv, ah, al,
        smem=(0,),
        scratch=scratch,
        flops=1e8,
        limit=8,
    )
    for pair in range(SWEEPS // 2):
        left, right = exchange(message)
        (t,) = call(inner_kernel, [state], t, winv, keep, wf, ah, al, flops=3e8, limit=8)
        if pair == SWEEPS // 2 - 1:
            break
        args = (t, message, left, right, winv, keep, wf, ah, al, bh, bl)
        if pair == 0:
            t, message, wf = call(
                second_kernel, [state, note, state], *args, scratch=scratch, flops=4e8, limit=8
            )
        else:
            t, message = call(sweep_kernel, [state, note], *args, scratch=scratch, flops=4e8, limit=8)
    ends_out = call(
        last_kernel,
        [piece] * GROUP,
        info, t, message, left, right, winv, keep, ah, al, bh, bl,
        smem=(0,),
        scratch=scratch,
        flops=1e8,
        limit=8,
    )
    there = {r: turn(ends_out[r], r) for r in (2, 1, 3)}
    velocity_new, trace = call(
        final_kernel,
        [arr(3, modes, points), arr(faces * NODES1, 3 * modes)],
        info, pos, ends_out[0], there[1], there[2], there[3], rhs0, rhs1, fh, fl,
        smem=(0, 1),
        hbm_out=(0, 1),
        scratch=[
            pltpu.VMEM((3, modes, NODES), F32),
            pltpu.VMEM((NODES, 3 * modes), F32),
            pltpu.VMEM((3, modes, points), F32),
            pltpu.VMEM((faces * NODES1, 3 * modes), F32),
            pltpu.SemaphoreType.DMA((4,)),
        ],
        flops=1e9,
        limit=7,
    )
    return velocity_new, trace.reshape(faces, NODES1, 3, modes)


def solution(mesh):
    return jax.shard_map(
        shards,
        mesh=mesh,
        in_specs=(
            P(None, "mode", "elem"),
            P(None, "elem"),
            P("elem", None, None),
            P("elem", None, None),
            P("elem", None),
            P("elem", None),
        ),
        out_specs=(P(None, "mode", "elem"), P("elem", None, None, "mode")),
        check_vma=False,
    )
```
